1024 devices in a mesh: dp: 4 (over x_hi, core), expert: 32 (over x_lo, z), tensor: 8 (over y).
Axes of the slice: x: 4 (x_hi: 2, x_lo: 2; x = x_hi * 2 + x_lo), y: 8, z: 16, core: 2. Of those that a mesh axis runs over, the one named last changes fastest.
Arguments:
- expert_partials: bfloat16 [4, 28672, 2048], P('dp', 'expert', 'tensor'), may hold values from -4096 to 4096
- token_counts: int32 [4, 4], P('dp'), may hold values from 256 to 2047
- expert_master: float32 [28672, 2048], P(('expert', 'dp'), 'tensor'), may hold values from -0.12 to 0.12
- expert_moment: float32 [28672, 2048], P(('expert', 'dp'), 'tensor'), may hold values from -6 to 6
- expert_second: float32 [28672, 2048], P(('expert', 'dp'), 'tensor'), may hold values from 0.01 to 4
- dense_partials: bfloat16 [128, 128, 8, 1024], P(('dp', 'expert'), None, 'tensor'), may hold values from -7 to 7
- dense_master: float32 [1048576], P(('dp', 'expert', 'tensor')), may hold values from -0.12 to 0.12
- dense_moment: float32 [1048576], P(('dp', 'expert', 'tensor')), may hold values from -6 to 6
- dense_second: float32 [1048576], P(('dp', 'expert', 'tensor')), may hold values from 0.01 to 4
Outputs:
- expert_weight: bfloat16 [28672, 2048], P('expert', 'tensor')
- expert_master_new: float32 [28672, 2048], P(('expert', 'dp'), 'tensor')
- expert_moment_new: float32 [28672, 2048], P(('expert', 'dp'), 'tensor')
- expert_second_new: float32 [28672, 2048], P(('expert', 'dp'), 'tensor')
- dense_weight: bfloat16 [128, 8, 1024], P(None, 'tensor')
- dense_master_new: float32 [1048576], P(('dp', 'expert', 'tensor'))
- dense_moment_new: float32 [1048576], P(('dp', 'expert', 'tensor'))
- dense_second_new: float32 [1048576], P(('dp', 'expert', 'tensor'))
The draws below stay inside these ranges and needn't reach their ends.
Inputs may be any that keep to these rules, and one draw needn't show every extreme that they name: token_counts[r, e] is the number of tokens of data replica r routed to expert e.
All inputs are finite; a program needn't handle non-finite values.
Results may differ from the reference program's by a relative error of at most 0.014.
Values may be sent and summed in bfloat16 or wider, within the bound.
A program may use at most 32 MiB of HBM per device.

```python
import math
import jax
import jax.numpy as jnp
from jax import lax

D = 7168
FF = 2048
EXPERTS = 4
DENSE_DEV = 1024
GROUPS = 128
DENSE = 1048576
N_DP = 4
N_TENSOR = 8


def plant(drawn, own_key, least, top_value):
    shape = drawn.shape
    place = [jax.random.randint(jax.random.fold_in(own_key, axis), (), 0, shape[axis]) for axis in range(len(shape))]
    drawn = drawn.at[tuple(place)].set(least)
    longest = shape.index(max(shape))
    place[longest] = (place[longest] + 1) % shape[longest]
    return drawn.at[tuple(place)].set(top_value)


def strengthened(entries, own_key, source, target, blocks, factor):
    owner, partner = [(jnp.arange(entries.shape[position]) // (entries.shape[position] // blocks)).reshape([-1 if axis == position else 1 for axis in range(entries.ndim)]) for position in (source, target)]
    chosen = jax.random.permutation(own_key, blocks)[partner]
    strong = (owner == chosen) | (owner == (partner + blocks // 2) % blocks)
    return jnp.where(strong, factor * entries, entries)


def block_levels(stream_key, shape, shards, smallest, top_value):
    factor_of = 1.0
    for dim, blocks in shards:
        heights = jax.random.uniform(jax.random.fold_in(jax.random.fold_in(stream_key, 6), dim), (blocks,), jnp.float32, smallest / len(shards), top_value / len(shards))
        factor_of = factor_of * jnp.repeat(jnp.exp(heights), shape[dim] // blocks).reshape((-1,) + (1,) * (len(shape) - 1 - dim))
    return factor_of


def centred(own_key, dims, deviation, limit, cuts=(), kind=jnp.bfloat16):
    gain = block_levels(own_key, dims, cuts, -0.22, 0.18) if cuts else 1.0
    array = jax.random.normal(own_key, dims, jnp.float32) * deviation * gain
    return jnp.minimum(jnp.maximum(array, -limit), limit).astype(kind)


def noise_with(key, shape, scale, bound, pieces, heavy, kind=jnp.bfloat16):
    result = scale * jax.random.normal(key, shape, jnp.float32)
    if pieces:
        result = result * block_levels(key, shape, pieces, -0.22, 0.18)
    return jnp.clip(strengthened(result, jax.random.fold_in(key, 3), *heavy), -bound, bound).astype(kind)


def setup_inputs(seed: int = 0) -> dict:
    splits = jax.random.split(jax.random.key(seed), 10)
    expert_partials = noise_with(splits[0], (N_DP, EXPERTS * D, FF), 512, 4096.0, ((0, 4), (1, 32), (2, 8)), (0, 1, 4, 2.0))
    token_counts = plant(jax.random.randint(splits[1], (N_DP, EXPERTS), 256, 2048), jax.random.fold_in(splits[1], 1), 256, 2047).astype(jnp.int32)
    expert_master = centred(splits[2], (EXPERTS * D, FF), 0.02, 0.12, ((0, 128), (1, 8)), jnp.float32)
    expert_moment = centred(splits[3], (EXPERTS * D, FF), 1.0, 6.0, ((0, 128), (1, 8)), jnp.float32)
    expert_second = jnp.clip(jnp.exp(math.log(4.0) - 5.9914646 * jax.random.uniform(splits[4], (EXPERTS * D, FF), jnp.float32) ** block_levels(splits[4], (EXPERTS * D, FF), ((0, 128), (1, 8)), -0.2, 0.2)), 0.01, 4.0)
    dense_partials = noise_with(splits[5], (GROUPS, GROUPS, N_TENSOR, DENSE_DEV), 0.3, 7.0, ((0, 128), (2, 8)), (0, 1, 128, 5.5))
    dense_master = centred(splits[6], (DENSE,), 0.02, 0.12, ((0, 1024),), jnp.float32)
    dense_moment = centred(splits[7], (DENSE,), 1.0, 6.0, ((0, 1024),), jnp.float32)
    dense_second = jnp.clip(jnp.exp(math.log(4.0) - 5.9914646 * jax.random.uniform(splits[8], (DENSE,), jnp.float32) ** block_levels(splits[8], (DENSE,), ((0, 1024),), -0.2, 0.2)), 0.01, 4.0)
    return dict(expert_partials=expert_partials, token_counts=token_counts, expert_master=expert_master, expert_moment=expert_moment, expert_second=expert_second, dense_partials=dense_partials, dense_master=dense_master, dense_moment=dense_moment, dense_second=dense_second)


beta_one = 0.9
beta_two = 0.95
epsilon = 1e-08
learn_rate = 0.001
weight_decay = 0.1
bias_one = 1.0 - 0.9 ** 10
bias_two = 1.0 - 0.95 ** 10

def adam_update(weight, moment, second, gradient):
    moment_new = beta_one * moment + (1.0 - beta_one) * gradient
    second_new = beta_two * second + (1.0 - beta_two) * gradient * gradient
    ratio = moment_new / bias_one / (jnp.sqrt(second_new / bias_two) + epsilon)
    weight_new = weight - learn_rate * (ratio + weight_decay * weight)
    return (weight_new, moment_new, second_new)

def reference(expert_partials, token_counts, expert_master, expert_moment, expert_second, dense_partials, dense_master, dense_moment, dense_second):
    counts = token_counts.astype(jnp.float32)
    gradient = jnp.zeros((EXPERTS, D, FF), jnp.float32)
    for replica in range(N_DP):
        block = expert_partials[replica].reshape(EXPERTS, D, FF).astype(jnp.float32)
        scaled = (block / counts[replica][:, None, None]).astype(jnp.bfloat16)
        scaled = lax.optimization_barrier(scaled)
        gradient = gradient + scaled.astype(jnp.float32)
    gradient = gradient.reshape(EXPERTS * D, FF)
    master_new, moment_new, second_new = adam_update(expert_master, expert_moment, expert_second, gradient)
    dense_gradient = lax.optimization_barrier(jnp.sum(dense_partials, axis=0, dtype=jnp.float32)).reshape(DENSE)
    dense_new, dense_moment_new, dense_second_new = adam_update(dense_master, dense_moment, dense_second, dense_gradient)
    dense_weight = dense_new.astype(jnp.bfloat16).reshape(GROUPS, N_TENSOR, DENSE_DEV)
    return (master_new.astype(jnp.bfloat16), master_new, moment_new, second_new, dense_weight, dense_new, dense_moment_new, dense_second_new)
```

```python
import functools

import jax
import jax.numpy as jnp
from jax import lax
from jax.experimental import pallas as pl
from jax.experimental.pallas import tpu as pltpu
from jax.sharding import PartitionSpec as P

MESH = pl.DeviceIdType.MESH
F32 = jnp.float32
BF16 = jnp.bfloat16

beta_one = 0.9
beta_two = 0.95
epsilon = 1e-08
learn_rate = 0.001
weight_decay = 0.1
bias_one = 1.0 - 0.9**10
bias_two = 1.0 - 0.95**10

NX, NZ, NP = 4, 16, 4
NB = NZ // NP
ROWS = 224
COLS = 256
PER_EXPERT = 8
PIECE = NB * 8
NEAR = [(dx, dq) for dx in (2, 1, 3, 0) for dq in (2, 1, 3, 0) if (dx, dq) != (0, 0)]


def adam_update(weight, moment, second, gradient):
    moment_new = beta_one * moment + (1.0 - beta_one) * gradient
    second_new = beta_two * second + (1.0 - beta_two) * gradient * gradient
    ratio = moment_new / bias_one / (jnp.sqrt(second_new / bias_two) + epsilon)
    weight_new = weight - learn_rate * (ratio + weight_decay * weight)
    return (weight_new, moment_new, second_new)


def at(offset, size, unit):
    return pl.ds(pl.multiple_of(offset, unit), size)


def exchange(
    partials, counts, master, moment, second, dense, dmaster, dmoment, dsecond,
    weight_out, master_out, moment_out, second_out, dweight_out, dmaster_out, dmoment_out, dsecond_out,
    counts_s, blocks, states, scaled, pair_in, cross_send, cross_in,
    dense_own, dense_in, tiles, pieces, near_in, far_buf, dstates, dnew, dweights, spread,
    load_sem, pair_send, pair_recv, near_send, near_recv, far_send, far_recv,
    cross_ss, cross_rs, gather_send, gather_recv, back_send, back_recv, known,
):
    dp, ex = lax.axis_index("dp"), lax.axis_index("expert")
    xh, c = dp // 2, dp % 2
    xl, z = ex // NZ, ex % NZ
    x = 2 * xh + xl
    zb, q = z // NP, z % NP
    mine = x * NP + q

    def device(x, z, c):
        return {"dp": (x // 2) * 2 + c, "expert": (x % 2) * NZ + z}

    pair = device(x, z, 1 - c)
    cross = device((x + 2) % NX, z, c)
    near = [device((x + dx) % NX, zb * NP + (q + dq) % NP, c) for dx, dq in NEAR]
    far = [device(x, (z + NP * d) % NZ, c) for d in range(1, NB)]

    def send(src, dst, ss, rs, to):
        return pltpu.make_async_remote_copy(
            src_ref=src, dst_ref=dst, send_sem=ss, recv_sem=rs, device_id=to, device_id_type=MESH
        )

    def block(index, slot, sem):
        return pltpu.make_async_copy(
            partials.at[at(index * ROWS, ROWS, 32)], blocks.at[pl.ds(slot * ROWS, ROWS)], load_sem.at[sem]
        )

    load_counts = pltpu.make_async_copy(counts, counts_s, load_sem.at[0])
    load_blocks = [
        block(2 * xh + 1 - c, 0, 1),
        block(2 * (1 - xh) + 1 - c, 1, 2),
        block(2 * (1 - xh) + c, 2, 3),
        block(2 * xh + c, 3, 4),
    ]
    load_dense = [
        pltpu.make_async_copy(
            dense.at[at((2 * h + c) * 32, 32, 32)], dense_own.at[pl.ds(h * 32, 32)], load_sem.at[5 + h]
        )
        for h in range(2)
    ]
    load_dstates = [
        pltpu.make_async_copy(ref, dstates.at[at(zb * 24 + 8 * i, 8, 8)], load_sem.at[7 + i])
        for i, ref in enumerate((dmaster, dmoment, dsecond))
    ]
    load_states = [
        pltpu.make_async_copy(ref, states.at[i], load_sem.at[10 + i])
        for i, ref in enumerate((master, moment, second))
    ]
    load_counts.start()
    for copy in load_dense + load_blocks + load_dstates + load_states:
        copy.start()

    barrier = pltpu.get_barrier_semaphore()
    greeted = [pair] + near + [far[0], far[-1]]
    for other in greeted:
        pl.semaphore_signal(barrier, inc=1, device_id=other, device_id_type=MESH)

    load_counts.wait()
    count = counts_s[0, ex // PER_EXPERT].astype(F32)
    inverse = 1.0 / jnp.full((1, COLS), count, F32)

    def scale(slot, start):
        rows = blocks[pl.ds(slot * ROWS + start, 32)].astype(F32) * inverse
        return rows.astype(BF16)

    load_blocks[0].wait()
    load_blocks[1].wait()

    def scale_step(i, carry):
        rows = pl.ds(pl.multiple_of(i * 32, 32), 32)
        scaled[rows] = (blocks[rows].astype(F32) * inverse).astype(BF16)
        return carry

    lax.fori_loop(0, 2 * ROWS // 32, scale_step, 0)

    pl.semaphore_wait(barrier, len(greeted))

    dense_pair = [
        send(
            dense.at[at((2 * h + 1 - c) * 32, 32, 32)], dense_in.at[pl.ds(h * 32, 32)],
            pair_send.at[h], pair_recv.at[h], pair,
        )
        for h in range(2)
    ]
    block_pair = [
        send(
            scaled.at[pl.ds(h * ROWS, ROWS)], pair_in.at[pl.ds(h * ROWS, ROWS)],
            pair_send.at[2 + h], pair_recv.at[2 + h], pair,
        )
        for h in range(2)
    ]
    for copy in dense_pair + block_pair[::-1]:
        copy.start()
    pl.semaphore_signal(known, inc=1, device_id=far[0], device_id_type=MESH)

    for copy in load_dense:
        copy.wait()
    for copy in dense_pair:
        copy.wait_recv()
    for xx in range(NX):
        rows = pl.ds(xx * NZ, NZ)
        total = dense_own[rows].astype(F32) + dense_in[rows].astype(F32)
        for s in range(8):
            tiles[pl.ds(xx * NZ * 8 + s, NZ, stride=8), :] = total[:, s * 128 : (s + 1) * 128]
    for xx in range(NX):
        for qq in range(NP):
            t = xx * NP + qq
            for half in range(NB // 2):
                two = [tiles[pl.ds((xx * NZ + NP * (2 * half + k) + qq) * 8, 8), :] for k in range(2)]
                pieces[pl.ds(t * PIECE + half * 16, 16), :] = jnp.concatenate(two, axis=0).astype(BF16)

    to_near = []
    for k, (dx, dq) in enumerate(NEAR):
        t = ((x + dx) % NX) * NP + (q + dq) % NP
        copy = send(
            pieces.at[at(t * PIECE, PIECE, 32)], near_in.at[pl.ds(k * PIECE, PIECE)],
            near_send.at[k], near_recv.at[k], near[k],
        )
        copy.start()
        to_near.append(copy)

    load_blocks[2].wait()
    block_pair[1].wait_recv()

    def cross_step(i, carry):
        off = pl.multiple_of(i * 32, 32)
        own = (blocks[pl.ds(pl.multiple_of(2 * ROWS + off, 32), 32)].astype(F32) * inverse).astype(BF16)
        other = pair_in[pl.ds(pl.multiple_of(ROWS + off, 32), 32)]
        cross_send[pl.ds(off, 32)] = (own.astype(F32) + other.astype(F32)).astype(BF16)
        return carry

    lax.fori_loop(0, ROWS // 32, cross_step, 0)
    to_cross = send(cross_send, cross_in, cross_ss.at[0], cross_rs.at[0], cross)
    to_cross.start()

    for copy in load_dstates:
        copy.wait()
    pl.semaphore_wait(known, 1)
    own_states = dstates.at[at(zb * 24, 24, 8)]
    to_states = [
        send(own_states, own_states, far_send.at[d], far_recv.at[d], far[d]) for d in range(NB - 1)
    ]
    for copy in to_states:
        copy.start()

    total = [tiles[at((x * NZ + NP * b + q) * 8, 8, 8), :] for b in range(NB)]
    total = jnp.concatenate(total, axis=0)
    for k, copy in enumerate(to_near):
        copy.wait_recv()
        total = total + near_in[pl.ds(k * PIECE, PIECE), :].astype(F32)
    far_own = far_buf.at[at(zb * PIECE, PIECE, 32)]
    far_own[...] = total.astype(BF16)
    to_far = [
        send(far_own, far_own, far_send.at[NB - 1 + d], far_recv.at[NB - 1 + d], far[d])
        for d in (1, 0, 2)
    ]
    for copy in to_far:
        copy.start()

    load_blocks[3].wait()
    block_pair[0].wait_recv()
    for copy in load_states:
        copy.wait()
    to_cross.wait_recv()

    def update_step(i, carry):
        off = pl.multiple_of(i * 32, 32)
        rows = pl.ds(off, 32)
        own = (blocks[pl.ds(pl.multiple_of(3 * ROWS + off, 32), 32)].astype(F32) * inverse).astype(BF16)
        gradient = own.astype(F32) + pair_in[rows].astype(F32) + cross_in[rows].astype(F32)
        new, moment_new, second_new = adam_update(states[0, rows], states[1, rows], states[2, rows], gradient)
        master_out[rows] = new
        moment_out[rows] = moment_new
        second_out[rows] = second_new
        weight_out[pl.ds(pl.multiple_of(dp * ROWS + off, 32), 32)] = new.astype(BF16)
        return carry

    lax.fori_loop(0, ROWS // 32, update_step, 0)
    own_weight = weight_out.at[at(dp * ROWS, ROWS, 32)]
    weight_cross = send(own_weight, own_weight, cross_ss.at[1], cross_rs.at[1], cross)
    weight_cross.start()
    weight_pair = send(own_weight, own_weight, cross_ss.at[2], cross_rs.at[2], pair)
    weight_pair.start()

    for copy in to_states + to_far:
        copy.wait_recv()
    dense_sum = jnp.zeros((PIECE, 128), F32)
    for b in range(NB):
        dense_sum = dense_sum + far_buf[pl.ds(b * PIECE, PIECE), :].astype(F32)
    news = []
    for b in range(NB):
        old = [dstates[pl.ds(b * 24 + 8 * i, 8), :] for i in range(3)]
        new = adam_update(*old, dense_sum[b * 8 : (b + 1) * 8])
        for i in range(3):
            dnew[pl.ds(b * 24 + 8 * i, 8), :] = new[i]
        news.append(new[0])
    own_piece = dweights.at[at(c * 512 + mine * PIECE, PIECE, 32)]
    own_piece[...] = jnp.concatenate(news, axis=0).astype(BF16)
    to_gather = [send(own_piece, own_piece, gather_send.at[k], gather_recv.at[k], near[k]) for k in range(len(NEAR))]
    for copy in to_gather:
        copy.start()
    for i, ref in enumerate((dmaster_out, dmoment_out, dsecond_out)):
        ref[...] = dnew[at(zb * 24 + 8 * i, 8, 8), :]

    weight_cross.wait_recv()
    cross_weight = weight_out.at[at((2 * (1 - xh) + c) * ROWS, ROWS, 32)]
    weight_on = send(cross_weight, cross_weight, cross_ss.at[3], cross_rs.at[3], pair)
    weight_on.start()

    def place(core, xx):
        first = pl.multiple_of(core * 512 + xx * NP * PIECE, 128)
        for qq in range(NP):
            piece = dweights[pl.ds(pl.multiple_of(first + qq * PIECE, 32), PIECE), :].astype(F32)
            for b in range(NB):
                spread[pl.ds((NP * b + qq) * 8, 8), :] = piece[b * 8 : (b + 1) * 8]
        to = at(((xx // 2) * 2 + core) * 32 + (xx % 2) * NZ, NZ, 16)
        for s in range(8):
            dweight_out[to, s * 128 : (s + 1) * 128] = spread[pl.ds(s, NZ, stride=8), :].astype(BF16)

    backs = []
    for n, dx in enumerate((0, 1, 3, 2)):
        for k, (ddx, dq) in enumerate(NEAR):
            if ddx == dx:
                to_gather[k].wait_recv()
        group = dweights.at[at(c * 512 + ((x - dx) % NX) * NP * PIECE, NP * PIECE, 128)]
        back = send(group, group, back_send.at[n], back_recv.at[n], pair)
        back.start()
        backs.append(back)
        place(c, (x - dx) % NX)
    for n, dx in enumerate((0, 1, 3, 2)):
        backs[n].wait_recv()
        place(1 - c, (x - dx) % NX)

    weight_pair.wait_recv()
    weight_on.wait_recv()
    for copy in (
        dense_pair + block_pair + to_near + [to_cross] + to_states + to_far
        + [weight_cross, weight_pair, weight_on] + to_gather + backs
    ):
        copy.wait_send()


def store(*refs):
    sources, outs, sem = refs[:8], refs[8:16], refs[16]
    copies = [pltpu.make_async_copy(s, o, sem.at[i]) for i, (s, o) in enumerate(zip(sources, outs))]
    for copy in copies:
        copy.start()
    for copy in copies:
        copy.wait()


def shards(
    expert_partials,
    token_counts,
    expert_master,
    expert_moment,
    expert_second,
    dense_partials,
    dense_master,
    dense_moment,
    dense_second,
):
    hbm = pl.BlockSpec(memory_space=pltpu.HBM)
    vmem = pl.BlockSpec(memory_space=pltpu.VMEM)
    dma = pltpu.SemaphoreType.DMA
    shapes = [
        ((4 * ROWS, COLS), BF16),
        ((ROWS, COLS), F32),
        ((ROWS, COLS), F32),
        ((ROWS, COLS), F32),
        ((128, 1024), BF16),
        ((8, 128), F32),
        ((8, 128), F32),
        ((8, 128), F32),
    ]
    n = len(NEAR)
    results = pl.pallas_call(
        exchange,
        out_shape=[pltpu.VMEM(s, d) for s, d in shapes],
        in_specs=[hbm] * 9,
        out_specs=[vmem] * 8,
        scratch_shapes=[
            pltpu.SMEM((1, 4), jnp.int32),
            pltpu.VMEM((4 * ROWS, COLS), BF16),
            pltpu.VMEM((3, ROWS, COLS), F32),
            pltpu.VMEM((2 * ROWS, COLS), BF16),
            pltpu.VMEM((2 * ROWS, COLS), BF16),
            pltpu.VMEM((ROWS, COLS), BF16),
            pltpu.VMEM((ROWS, COLS), BF16),
            pltpu.VMEM((64, 1024), BF16),
            pltpu.VMEM((64, 1024), BF16),
            pltpu.VMEM((512, 128), F32),
            pltpu.VMEM((512, 128), BF16),
            pltpu.VMEM((n * PIECE, 128), BF16),
            pltpu.VMEM((NB * PIECE, 128), BF16),
            pltpu.VMEM((NB * 24, 128), F32),
            pltpu.VMEM((NB * 24, 128), F32),
            pltpu.VMEM((1024, 128), BF16),
            pltpu.VMEM((128, 128), F32),
            dma((13,)),
            dma((4,)),
            dma((4,)),
            dma((n,)),
            dma((n,)),
            dma((6,)),
            dma((6,)),
            dma((4,)),
            dma((4,)),
            dma((n,)),
            dma((n,)),
            dma((4,)),
            dma((4,)),
            pltpu.SemaphoreType.REGULAR,
        ],
        compiler_params=pltpu.CompilerParams(
            collective_id=0, has_side_effects=True, vmem_limit_bytes=24 * 2**20
        ),
        name="exchange",
    )(
        expert_partials.reshape(4 * ROWS, COLS),
        token_counts,
        expert_master,
        expert_moment,
        expert_second,
        dense_partials.reshape(128, 1024),
        dense_master.reshape(8, 128),
        dense_moment.reshape(8, 128),
        dense_second.reshape(8, 128),
    )
    outs = pl.pallas_call(
        store,
        out_shape=[jax.ShapeDtypeStruct(s, d) for s, d in shapes],
        in_specs=[vmem] * 8,
        out_specs=[hbm] * 8,
        scratch_shapes=[dma((8,))],
        compiler_params=pltpu.CompilerParams(vmem_limit_bytes=8 * 2**20),
        name="store",
    )(*results)
    outs = list(outs)
    outs[4] = outs[4].reshape(128, 1, 1024)
    for i in (5, 6, 7):
        outs[i] = outs[i].reshape(1024)
    return tuple(outs)


def solution(mesh):
    return jax.shard_map(
        shards,
        mesh=mesh,
        in_specs=(
            P("dp", "expert", "tensor"),
            P("dp", None),
            P(("expert", "dp"), "tensor"),
            P(("expert", "dp"), "tensor"),
            P(("expert", "dp"), "tensor"),
            P(("dp", "expert"), None, "tensor", None),
            P(("dp", "expert", "tensor")),
            P(("dp", "expert", "tensor")),
            P(("dp", "expert", "tensor")),
        ),
        out_specs=(
            P("expert", "tensor"),
            P(("expert", "dp"), "tensor"),
            P(("expert", "dp"), "tensor"),
            P(("expert", "dp"), "tensor"),
            P(None, "tensor", None),
            P(("dp", "expert", "tensor")),
            P(("dp", "expert", "tensor")),
            P(("dp", "expert", "tensor")),
        ),
        check_vma=False,
    )
```

```python
import functools

import jax
import jax.numpy as jnp
from jax import lax
from jax.experimental import pallas as pl
from jax.experimental.pallas import tpu as pltpu
from jax.sharding import PartitionSpec as P

MESH = pl.DeviceIdType.MESH
F32 = jnp.float32
BF16 = jnp.bfloat16

beta_one = 0.9
beta_two = 0.95
epsilon = 1e-08
learn_rate = 0.001
weight_decay = 0.1
bias_one = 1.0 - 0.9**10
bias_two = 1.0 - 0.95**10

NX, NZ, NQ = 4, 16, 4
NB = NZ // NQ
ROWS = 224
COLS = 256
PER_EXPERT = 8
PIECE = NB * 8
DX = (2, 1, 3, 0)
DZ = (-2, 1, -1, 0)
NEAR = [(dx, dz) for dx in DX for dz in DZ if (dx, dz) != (0, 0)]


def adam_update(weight, moment, second, gradient):
    moment_new = beta_one * moment + (1.0 - beta_one) * gradient
    second_new = beta_two * second + (1.0 - beta_two) * gradient * gradient
    ratio = moment_new / bias_one / (jnp.sqrt(second_new / bias_two) + epsilon)
    weight_new = weight - learn_rate * (ratio + weight_decay * weight)
    return (weight_new, moment_new, second_new)


def at(offset, size, unit):
    return pl.ds(pl.multiple_of(offset, unit), size)


def exchange(
    partials, counts, master, moment, second, dense, dmaster, dmoment, dsecond,
    weight_out, master_out, moment_out, second_out, dweight_out, dmaster_out, dmoment_out, dsecond_out,
    counts_s, blocks, states, scaled, pair_in, cross_send, cross_in,
    dense_own, dense_in, tiles, pieces, near_in, far_buf, dstates, dnew, dweights, spread,
    load_sem, pair_send, pair_recv, near_send, near_recv, far_send, far_recv,
    cross_ss, cross_rs, gather_send, gather_recv, back_send, back_recv, known,
):
    dp, ex = lax.axis_index("dp"), lax.axis_index("expert")
    xh, c = dp // 2, dp % 2
    xl, z = ex // NZ, ex % NZ
    x = 2 * xh + xl
    zb, q = z // NQ, z % NQ
    sign = 1 - 2 * c
    columns = [(x + dx) % NX for dx in DX]

    def device(x, z, c):
        return {"dp": ((x % NX) // 2) * 2 + c, "expert": (x % 2) * NZ + z % NZ}

    def along(dz):
        return (z + sign * dz + NZ) % NZ

    pair = device(x, z, 1 - c)
    cross = device(x + 2, z, c)
    near = [device(x + dx, along(dz), c) for dx, dz in NEAR]
    near_back = [device(x + NX - dx, along(-dz), c) for dx, dz in NEAR]
    far = [device(x, z + NQ * d, c) for d in range(1, NB)]

    def send(src, dst, ss, rs, to):
        return pltpu.make_async_remote_copy(
            src_ref=src, dst_ref=dst, send_sem=ss, recv_sem=rs, device_id=to, device_id_type=MESH
        )

    def dense_rows(column, core):
        return at(((column // 2) * 2 + core) * 32 + (column % 2) * NZ, NZ, 16)

    def block(index, slot, sem):
        return pltpu.make_async_copy(
            partials.at[at(index * ROWS, ROWS, 32)], blocks.at[pl.ds(slot * ROWS, ROWS)], load_sem.at[sem]
        )

    load_counts = pltpu.make_async_copy(counts, counts_s, load_sem.at[0])
    load_blocks = [
        block(2 * xh + 1 - c, 0, 1),
        block(2 * (1 - xh) + 1 - c, 1, 2),
        block(2 * (1 - xh) + c, 2, 3),
        block(2 * xh + c, 3, 4),
    ]
    load_dense = [
        pltpu.make_async_copy(
            dense.at[dense_rows(column, c)], dense_own.at[pl.ds(n * NZ, NZ)], load_sem.at[5 + n]
        )
        for n, column in enumerate(columns)
    ]
    load_dstates = [
        pltpu.make_async_copy(ref, dstates.at[at(zb * 24 + 8 * i, 8, 8)], load_sem.at[9 + i])
        for i, ref in enumerate((dmaster, dmoment, dsecond))
    ]
    load_states = [
        pltpu.make_async_copy(ref, states.at[i], load_sem.at[12 + i])
        for i, ref in enumerate((master, moment, second))
    ]

    barrier = pltpu.get_barrier_semaphore()
    greeted = near_back + [pair, far[0], far[-1]]
    for other in greeted:
        pl.semaphore_signal(barrier, inc=1, device_id=other, device_id_type=MESH)

    load_counts.start()
    for copy in load_blocks[:2] + load_dense + load_dstates + load_blocks[2:] + load_states:
        copy.start()

    load_counts.wait()
    count = counts_s[0, ex // PER_EXPERT].astype(F32)
    inverse = 1.0 / jnp.full((1, COLS), count, F32)
    load_blocks[0].wait()
    load_blocks[1].wait()

    def scale_step(i, carry):
        rows = pl.ds(pl.multiple_of(i * 64, 64), 64)
        scaled[rows] = (blocks[rows].astype(F32) * inverse).astype(BF16)
        return carry

    lax.fori_loop(0, 2 * ROWS // 64, scale_step, 0)
    for copy in load_dstates:
        copy.wait()

    pl.semaphore_wait(barrier, len(near) + 3)

    dense_pair = [
        send(
            dense.at[dense_rows(column, 1 - c)], dense_in.at[pl.ds(n * NZ, NZ)],
            pair_send.at[n], pair_recv.at[n], pair,
        )
        for n, column in enumerate(columns)
    ]
    block_pair = [
        send(
            scaled.at[pl.ds(h * ROWS, ROWS)], pair_in.at[pl.ds(h * ROWS, ROWS)],
            pair_send.at[4 + h], pair_recv.at[4 + h], pair,
        )
        for h in range(2)
    ]
    for copy in dense_pair + block_pair[::-1]:
        copy.start()
    pl.semaphore_signal(known, inc=1, device_id=far[0], device_id_type=MESH)
    own_states = dstates.at[at(zb * 24, 24, 8)]
    to_states = [
        send(own_states, own_states, far_send.at[d], far_recv.at[d], far[d]) for d in range(NB - 1)
    ]
    to_states[0].start()
    to_states[2].start()

    to_near = []
    for n, dx in enumerate(DX):
        load_dense[n].wait()
        dense_pair[n].wait_recv()
        rows = pl.ds(n * NZ, NZ)
        total = dense_own[rows].astype(F32) + dense_in[rows].astype(F32)
        for s in range(8):
            tiles[pl.ds(n * NZ * 8 + s, NZ, stride=8), :] = total[:, s * 128 : (s + 1) * 128]
        for qq in range(NQ):
            for half in range(NB // 2):
                two = [tiles[pl.ds((n * NZ + NQ * (2 * half + k) + qq) * 8, 8), :] for k in range(2)]
                pieces[pl.ds((n * NQ + qq) * PIECE + half * 16, 16), :] = jnp.concatenate(two, axis=0).astype(BF16)
        for k, (ddx, dz) in enumerate(NEAR):
            if ddx == dx:
                copy = send(
                    pieces.at[at((n * NQ + along(dz) % NQ) * PIECE, PIECE, 32)],
                    near_in.at[pl.ds(k * PIECE, PIECE)],
                    near_send.at[k], near_recv.at[k], near[k],
                )
                copy.start()
                to_near.append(copy)

    pl.semaphore_wait(known, 1)
    to_states[1].start()

    load_blocks[2].wait()
    block_pair[1].wait_recv()

    def cross_step(i, carry):
        off = pl.multiple_of(i * 32, 32)
        own = (blocks[pl.ds(pl.multiple_of(2 * ROWS + off, 32), 32)].astype(F32) * inverse).astype(BF16)
        other = pair_in[pl.ds(pl.multiple_of(ROWS + off, 32), 32)]
        cross_send[pl.ds(off, 32)] = (own.astype(F32) + other.astype(F32)).astype(BF16)
        return carry

    lax.fori_loop(0, ROWS // 32, cross_step, 0)
    to_cross = send(cross_send, cross_in, cross_ss.at[0], cross_rs.at[0], cross)

    total = [tiles[at((3 * NZ + NQ * b + q) * 8, 8, 8), :] for b in range(NB)]
    total = jnp.concatenate(total, axis=0)
    for k in reversed(range(len(NEAR))):
        if k == 3:
            to_cross.start()
        to_near[k].wait_recv()
        total = total + near_in[pl.ds(k * PIECE, PIECE), :].astype(F32)
    far_own = far_buf.at[at(zb * PIECE, PIECE, 32)]
    far_own[...] = total.astype(BF16)
    to_far = [
        send(far_own, far_own, far_send.at[NB - 1 + d], far_recv.at[NB - 1 + d], far[d])
        for d in (1, 0, 2)
    ]
    for copy in to_far:
        copy.start()

    load_blocks[3].wait()
    block_pair[0].wait_recv()
    for copy in load_states:
        copy.wait()
    for copy in dense_pair + block_pair + to_near:
        copy.wait_send()
    to_cross.wait_recv()

    def update_step(i, carry):
        off = pl.multiple_of(i * 32, 32)
        rows = pl.ds(off, 32)
        own = (blocks[pl.ds(pl.multiple_of(3 * ROWS + off, 32), 32)].astype(F32) * inverse).astype(BF16)
        gradient = own.astype(F32) + pair_in[rows].astype(F32) + cross_in[rows].astype(F32)
        new, moment_new, second_new = adam_update(states[0, rows], states[1, rows], states[2, rows], gradient)
        master_out[rows] = new
        moment_out[rows] = moment_new
        second_out[rows] = second_new
        weight_out[pl.ds(pl.multiple_of(dp * ROWS + off, 32), 32)] = new.astype(BF16)
        return carry

    lax.fori_loop(0, ROWS // 32, update_step, 0)
    own_weight = weight_out.at[at(dp * ROWS, ROWS, 32)]
    weight_cross = send(own_weight, own_weight, cross_ss.at[1], cross_rs.at[1], cross)
    weight_cross.start()
    weight_pair = send(own_weight, own_weight, cross_ss.at[2], cross_rs.at[2], pair)
    weight_pair.start()

    for copy in to_states:
        copy.wait()
    to_cross.wait_send()
    for copy in to_far[::-1]:
        copy.wait_recv()
    dense_sum = jnp.zeros((PIECE, 128), F32)
    for b in range(NB):
        dense_sum = dense_sum + far_buf[pl.ds(b * PIECE, PIECE), :].astype(F32)
    news = []
    for b in range(NB):
        old = [dstates[pl.ds(b * 24 + 8 * i, 8), :] for i in range(3)]
        new = adam_update(*old, dense_sum[b * 8 : (b + 1) * 8])
        for i in range(3):
            dnew[pl.ds(b * 24 + 8 * i, 8), :] = new[i]
        news.append(new[0])
    own_piece = dweights.at[at(c * 512 + (x * NQ + q) * PIECE, PIECE, 32)]
    own_piece[...] = jnp.concatenate(news, axis=0).astype(BF16)
    to_gather = [send(own_piece, own_piece, gather_send.at[k], gather_recv.at[k], near[k]) for k in range(len(NEAR))]
    for copy in to_gather:
        copy.start()
    for i, ref in enumerate((dmaster_out, dmoment_out, dsecond_out)):
        ref[...] = dnew[at(zb * 24 + 8 * i, 8, 8), :]
    for copy in to_far:
        copy.wait_send()

    weight_cross.wait()
    weight_pair.wait_send()
    cross_weight = weight_out.at[at((2 * (1 - xh) + c) * ROWS, ROWS, 32)]
    weight_on = send(cross_weight, cross_weight, cross_ss.at[3], cross_rs.at[3], pair)
    weight_on.start()

    def place(core, column, slot):
        first = pl.multiple_of(core * 512 + column * NQ * PIECE, 128)
        for qq in range(NQ):
            piece = dweights[pl.ds(pl.multiple_of(first + qq * PIECE, 32), PIECE), :].astype(F32)
            for b in range(NB):
                spread[pl.ds((slot * NZ + NQ * b + qq) * 8, 8), :] = piece[b * 8 : (b + 1) * 8]
        to = dense_rows(column, core)
        for s in range(8):
            row = spread[pl.ds(slot * NZ * 8 + s, NZ, stride=8), :]
            dweight_out[to, s * 128 : (s + 1) * 128] = row.astype(BF16)

    order = (3, 1, 2, 0)
    backs = []
    for n in order:
        dx = (NX - DX[n]) % NX
        for k, (ddx, dz) in enumerate(NEAR):
            if ddx == dx:
                to_gather[k].wait_recv()
        group = dweights.at[at(c * 512 + columns[n] * NQ * PIECE, NQ * PIECE, 128)]
        back = send(group, group, back_send.at[n], back_recv.at[n], pair)
        back.start()
        backs.append(back)
        place(c, columns[n], n)
    for copy in to_gather:
        copy.wait_send()
    weight_pair.wait_recv()
    weight_on.wait()
    for n, back in zip(order, backs):
        back.wait_recv()
        place(1 - c, columns[n], 4 + n)
    for back in backs:
        back.wait_send()


def store(*refs):
    sources, outs, sem = refs[:8], refs[8:16], refs[16]
    copies = [pltpu.make_async_copy(s, o, sem.at[i]) for i, (s, o) in enumerate(zip(sources, outs))]
    for copy in copies:
        copy.start()
    for copy in copies:
        copy.wait()


def shards(
    expert_partials,
    token_counts,
    expert_master,
    expert_moment,
    expert_second,
    dense_partials,
    dense_master,
    dense_moment,
    dense_second,
):
    hbm = pl.BlockSpec(memory_space=pltpu.HBM)
    vmem = pl.BlockSpec(memory_space=pltpu.VMEM)
    dma = pltpu.SemaphoreType.DMA
    shapes = [
        ((4 * ROWS, COLS), BF16),
        ((ROWS, COLS), F32),
        ((ROWS, COLS), F32),
        ((ROWS, COLS), F32),
        ((128, 1024), BF16),
        ((8, 128), F32),
        ((8, 128), F32),
        ((8, 128), F32),
    ]
    n = len(NEAR)
    results = pl.pallas_call(
        exchange,
        out_shape=[pltpu.VMEM(s, d) for s, d in shapes],
        in_specs=[hbm] * 9,
        out_specs=[vmem] * 8,
        scratch_shapes=[
            pltpu.SMEM((1, 4), jnp.int32),
            pltpu.VMEM((4 * ROWS, COLS), BF16),
            pltpu.VMEM((3, ROWS, COLS), F32),
            pltpu.VMEM((2 * ROWS, COLS), BF16),
            pltpu.VMEM((2 * ROWS, COLS), BF16),
            pltpu.VMEM((ROWS, COLS), BF16),
            pltpu.VMEM((ROWS, COLS), BF16),
            pltpu.VMEM((64, 1024), BF16),
            pltpu.VMEM((64, 1024), BF16),
            pltpu.VMEM((512, 128), F32),
            pltpu.VMEM((512, 128), BF16),
            pltpu.VMEM((n * PIECE, 128), BF16),
            pltpu.VMEM((NB * PIECE, 128), BF16),
            pltpu.VMEM((NB * 24, 128), F32),
            pltpu.VMEM((NB * 24, 128), F32),
            pltpu.VMEM((1024, 128), BF16),
            pltpu.VMEM((1024, 128), F32),
            dma((15,)),
            dma((6,)),
            dma((6,)),
            dma((n,)),
            dma((n,)),
            dma((6,)),
            dma((6,)),
            dma((4,)),
            dma((4,)),
            dma((n,)),
            dma((n,)),
            dma((4,)),
            dma((4,)),
            pltpu.SemaphoreType.REGULAR,
        ],
        compiler_params=pltpu.CompilerParams(
            collective_id=0, has_side_effects=True, vmem_limit_bytes=56 * 2**20
        ),
        name="exchange",
    )(
        expert_partials.reshape(4 * ROWS, COLS),
        token_counts,
        expert_master,
        expert_moment,
        expert_second,
        dense_partials.reshape(128, 1024),
        dense_master.reshape(8, 128),
        dense_moment.reshape(8, 128),
        dense_second.reshape(8, 128),
    )
    outs = pl.pallas_call(
        store,
        out_shape=[jax.ShapeDtypeStruct(s, d) for s, d in shapes],
        in_specs=[vmem] * 8,
        out_specs=[hbm] * 8,
        scratch_shapes=[dma((8,))],
        compiler_params=pltpu.CompilerParams(vmem_limit_bytes=8 * 2**20),
        name="store",
    )(*results)
    outs = list(outs)
    outs[4] = outs[4].reshape(128, 1, 1024)
    for i in (5, 6, 7):
        outs[i] = outs[i].reshape(1024)
    return tuple(outs)


def solution(mesh):
    return jax.shard_map(
        shards,
        mesh=mesh,
        in_specs=(
            P("dp", "expert", "tensor"),
            P("dp", None),
            P(("expert", "dp"), "tensor"),
            P(("expert", "dp"), "tensor"),
            P(("expert", "dp"), "tensor"),
            P(("dp", "expert"), None, "tensor", None),
            P(("dp", "expert", "tensor")),
            P(("dp", "expert", "tensor")),
            P(("dp", "expert", "tensor")),
        ),
        out_specs=(
            P("expert", "tensor"),
            P(("expert", "dp"), "tensor"),
            P(("expert", "dp"), "tensor"),
            P(("expert", "dp"), "tensor"),
            P(None, "tensor", None),
            P(("dp", "expert", "tensor")),
            P(("dp", "expert", "tensor")),
            P(("dp", "expert", "tensor")),
        ),
        check_vma=False,
    )
```

```python
import functools

import jax
import jax.numpy as jnp
from jax import lax
from jax.experimental import pallas as pl
from jax.experimental.pallas import tpu as pltpu
from jax.sharding import PartitionSpec as P

MESH = pl.DeviceIdType.MESH
F32 = jnp.float32
BF16 = jnp.bfloat16

beta_one = 0.9
beta_two = 0.95
epsilon = 1e-08
learn_rate = 0.001
weight_decay = 0.1
bias_one = 1.0 - 0.9**10
bias_two = 1.0 - 0.95**10

NX, NZ, NQ = 4, 16, 4
NB = NZ // NQ
ROWS = 224
COLS = 256
PER_EXPERT = 8
PIECE = NB * 8
DX = (2, 1, 3, 0)
DZ = (-2, 1, -1, 0)
GROUPS = ((0,), (1, 2), (3,))
NEAR = [(DX[n], dz) for group in GROUPS for dz in DZ for n in group if (DX[n], dz) != (0, 0)]


def adam_update(weight, moment, second, gradient):
    moment_new = beta_one * moment + (1.0 - beta_one) * gradient
    second_new = beta_two * second + (1.0 - beta_two) * gradient * gradient
    ratio = moment_new / bias_one / (jnp.sqrt(second_new / bias_two) + epsilon)
    weight_new = weight - learn_rate * (ratio + weight_decay * weight)
    return (weight_new, moment_new, second_new)


def at(offset, size, unit):
    return pl.ds(pl.multiple_of(offset, unit), size)


def exchange(
    partials, counts, master, moment, second, dense, dmaster, dmoment, dsecond,
    weight_out, master_out, moment_out, second_out, dweight_out, dmaster_out, dmoment_out, dsecond_out,
    counts_s, blocks, states, scaled, pair_in, cross_send, cross_in,
    dense_own, dense_out, dense_in, tiles, pieces, near_in, far_buf, dstates, dnew, dweights, spread,
    load_sem, pair_send, pair_recv, near_send, near_recv, far_send, far_recv,
    cross_ss, cross_rs, gather_send, gather_recv, back_send, back_recv, known, pair_in_kernel, all_in_kernel,
):
    dp, ex = lax.axis_index("dp"), lax.axis_index("expert")
    xh, c = dp // 2, dp % 2
    xl, z = ex // NZ, ex % NZ
    x = 2 * xh + xl
    zb, q = z // NQ, z % NQ
    sign = 1 - 2 * c
    columns = [(x + dx) % NX for dx in DX]

    def device(x, z, c):
        return {"dp": ((x % NX) // 2) * 2 + c, "expert": (x % 2) * NZ + z % NZ}

    def along(dz):
        return (z + sign * dz + NZ) % NZ

    pair = device(x, z, 1 - c)
    cross = device(x + 2, z, c)
    near = [device(x + dx, along(dz), c) for dx, dz in NEAR]
    near_back = [device(x + NX - dx, along(-dz), 1) for dx, dz in NEAR]
    far = [device(x, z + NQ * d, c) for d in range(1, NB)]

    def send(src, dst, ss, rs, to):
        return pltpu.make_async_remote_copy(
            src_ref=src, dst_ref=dst, send_sem=ss, recv_sem=rs, device_id=to, device_id_type=MESH
        )

    def dense_rows(column, core):
        return at(((column // 2) * 2 + core) * 32 + (column % 2) * NZ, NZ, 16)

    def block(index, slot, sem):
        return pltpu.make_async_copy(
            partials.at[at(index * ROWS, ROWS, 32)], blocks.at[pl.ds(slot * ROWS, ROWS)], load_sem.at[sem]
        )

    load_counts = pltpu.make_async_copy(counts, counts_s, load_sem.at[0])
    load_blocks = [
        block(2 * xh + 1 - c, 0, 1),
        block(2 * (1 - xh) + 1 - c, 1, 2),
        block(2 * (1 - xh) + c, 2, 3),
        block(2 * xh + c, 3, 4),
    ]
    load_dense = [
        pltpu.make_async_copy(
            dense.at[dense_rows(column, c)], dense_own.at[pl.ds(n * NZ, NZ)], load_sem.at[5 + n]
        )
        for n, column in enumerate(columns)
    ]
    load_out = [
        pltpu.make_async_copy(
            dense.at[dense_rows(column, 1 - c)], dense_out.at[pl.ds(n * NZ, NZ)], load_sem.at[15 + n]
        )
        for n, column in enumerate(columns)
    ]
    load_dstates = [
        pltpu.make_async_copy(ref, dstates.at[at(zb * 24 + 8 * i, 8, 8)], load_sem.at[9 + i])
        for i, ref in enumerate((dmaster, dmoment, dsecond))
    ]
    load_states = [
        pltpu.make_async_copy(ref, states.at[i], load_sem.at[12 + i])
        for i, ref in enumerate((master, moment, second))
    ]

    barrier = pltpu.get_barrier_semaphore()

    @pl.when(c == 1)
    def _():
        pl.semaphore_signal(barrier, inc=1, device_id=pair, device_id_type=MESH)

    greeted = near_back + [device(x, z + NQ, 1), device(x, z + NZ - NQ, 1)]
    for other in greeted:
        pl.semaphore_signal(barrier, inc=1, device_id=other, device_id_type=MESH)

    for copy in load_out + load_dense + [load_counts] + load_blocks + load_dstates + load_states:
        copy.start()

    @pl.when(c == 0)
    def _():
        pl.semaphore_wait(barrier, 1)
        pl.semaphore_signal(pair_in_kernel, inc=1, device_id=pair, device_id_type=MESH)

    @pl.when(c == 1)
    def _():
        pl.semaphore_wait(pair_in_kernel, 1)

    dense_pair = [
        send(
            dense_out.at[pl.ds(n * NZ, NZ)], dense_in.at[pl.ds(n * NZ, NZ)],
            pair_send.at[n], pair_recv.at[n], pair,
        )
        for n, column in enumerate(columns)
    ]
    block_pair = [
        send(
            scaled.at[pl.ds(h * ROWS, ROWS)], pair_in.at[pl.ds(h * ROWS, ROWS)],
            pair_send.at[4 + h], pair_recv.at[4 + h], pair,
        )
        for h in range(2)
    ]
    for load, copy in zip(load_out, dense_pair):
        load.wait()
        copy.start()

    load_counts.wait()
    count = counts_s[0, ex // PER_EXPERT].astype(F32)
    inverse = 1.0 / jnp.full((1, COLS), count, F32)
    load_blocks[0].wait()
    load_blocks[1].wait()

    def scale_step(i, carry):
        rows = pl.ds(pl.multiple_of(i * 64, 64), 64)
        scaled[rows] = (blocks[rows].astype(F32) * inverse).astype(BF16)
        return carry

    lax.fori_loop(0, 2 * ROWS // 64, scale_step, 0)
    for copy in block_pair[::-1]:
        copy.start()

    def sum_column(n):
        load_dense[n].wait()
        dense_pair[n].wait_recv()
        rows = pl.ds(n * NZ, NZ)
        total = dense_own[rows].astype(F32) + dense_in[rows].astype(F32)
        for s in range(8):
            tiles[pl.ds(n * NZ * 8 + s, NZ, stride=8), :] = total[:, s * 128 : (s + 1) * 128]
        for qq in range(NQ):
            for half in range(NB // 2):
                two = [tiles[pl.ds((n * NZ + NQ * (2 * half + k) + qq) * 8, 8), :] for k in range(2)]
                pieces[pl.ds((n * NQ + qq) * PIECE + half * 16, 16), :] = jnp.concatenate(two, axis=0).astype(BF16)

    for n in range(NX):
        sum_column(n)

    @pl.when(c == 1)
    def _():
        pl.semaphore_wait(barrier, 2 * len(greeted))
        pl.semaphore_signal(all_in_kernel, inc=1, device_id=pair, device_id_type=MESH)

    @pl.when(c == 0)
    def _():
        pl.semaphore_wait(all_in_kernel, 1)

    to_near = []
    for group in GROUPS:
        for k, (dx, dz) in enumerate(NEAR):
            if DX.index(dx) in group:
                copy = send(
                    pieces.at[at((DX.index(dx) * NQ + along(dz) % NQ) * PIECE, PIECE, 32)],
                    near_in.at[pl.ds(k * PIECE, PIECE)],
                    near_send.at[k], near_recv.at[k], near[k],
                )
                copy.start()
                to_near.append(copy)

    pl.semaphore_signal(known, inc=1, device_id=far[0], device_id_type=MESH)
    for copy in load_dstates:
        copy.wait()
    own_states = dstates.at[at(zb * 24, 24, 8)]
    to_states = [
        send(own_states, own_states, far_send.at[d], far_recv.at[d], far[d]) for d in range(NB - 1)
    ]
    to_states[0].start()
    to_states[2].start()

    load_blocks[2].wait()
    block_pair[1].wait_recv()

    def cross_step(i, carry):
        off = pl.multiple_of(i * 32, 32)
        own = (blocks[pl.ds(pl.multiple_of(2 * ROWS + off, 32), 32)].astype(F32) * inverse).astype(BF16)
        other = pair_in[pl.ds(pl.multiple_of(ROWS + off, 32), 32)]
        cross_send[pl.ds(off, 32)] = (own.astype(F32) + other.astype(F32)).astype(BF16)
        return carry

    lax.fori_loop(0, ROWS // 32, cross_step, 0)
    pl.semaphore_wait(known, 1)
    to_states[1].start()
    to_cross = send(cross_send, cross_in, cross_ss.at[0], cross_rs.at[0], cross)

    total = [tiles[at((3 * NZ + NQ * b + q) * 8, 8, 8), :] for b in range(NB)]
    total = jnp.concatenate(total, axis=0)
    for k in reversed(range(len(NEAR))):
        if k == 3:
            to_cross.start()
        to_near[k].wait_recv()
        total = total + near_in[pl.ds(k * PIECE, PIECE), :].astype(F32)
    far_own = far_buf.at[at(zb * PIECE, PIECE, 32)]
    far_own[...] = total.astype(BF16)
    to_far = [
        send(far_own, far_own, far_send.at[NB - 1 + d], far_recv.at[NB - 1 + d], far[d])
        for d in (1, 0, 2)
    ]
    for copy in to_far:
        copy.start()

    load_blocks[3].wait()
    block_pair[0].wait_recv()
    for copy in load_states:
        copy.wait()
    for copy in dense_pair + block_pair + to_near:
        copy.wait_send()
    to_cross.wait_recv()

    def update_step(i, carry):
        off = pl.multiple_of(i * 32, 32)
        rows = pl.ds(off, 32)
        own = (blocks[pl.ds(pl.multiple_of(3 * ROWS + off, 32), 32)].astype(F32) * inverse).astype(BF16)
        gradient = own.astype(F32) + pair_in[rows].astype(F32) + cross_in[rows].astype(F32)
        new, moment_new, second_new = adam_update(states[0, rows], states[1, rows], states[2, rows], gradient)
        master_out[rows] = new
        moment_out[rows] = moment_new
        second_out[rows] = second_new
        weight_out[pl.ds(pl.multiple_of(dp * ROWS + off, 32), 32)] = new.astype(BF16)
        return carry

    lax.fori_loop(0, ROWS // 32, update_step, 0)
    own_weight = weight_out.at[at(dp * ROWS, ROWS, 32)]
    weight_cross = send(own_weight, own_weight, cross_ss.at[1], cross_rs.at[1], cross)
    weight_cross.start()
    weight_pair = send(own_weight, own_weight, cross_ss.at[2], cross_rs.at[2], pair)
    weight_pair.start()

    for copy in to_states:
        copy.wait()
    to_cross.wait_send()
    for copy in to_far[::-1]:
        copy.wait_recv()
    dense_sum = jnp.zeros((PIECE, 128), F32)
    for b in range(NB):
        dense_sum = dense_sum + far_buf[pl.ds(b * PIECE, PIECE), :].astype(F32)
    news = []
    for b in range(NB):
        old = [dstates[pl.ds(b * 24 + 8 * i, 8), :] for i in range(3)]
        new = adam_update(*old, dense_sum[b * 8 : (b + 1) * 8])
        for i in range(3):
            dnew[pl.ds(b * 24 + 8 * i, 8), :] = new[i]
        news.append(new[0])
    own_piece = dweights.at[at(c * 512 + (x * NQ + q) * PIECE, PIECE, 32)]
    own_piece[...] = jnp.concatenate(news, axis=0).astype(BF16)
    to_gather = [send(own_piece, own_piece, gather_send.at[k], gather_recv.at[k], near[k]) for k in range(len(NEAR))]
    for copy in to_gather:
        copy.start()
    for i, ref in enumerate((dmaster_out, dmoment_out, dsecond_out)):
        ref[...] = dnew[at(zb * 24 + 8 * i, 8, 8), :]
    for copy in to_far:
        copy.wait_send()

    weight_cross.wait()
    weight_pair.wait_send()
    cross_weight = weight_out.at[at((2 * (1 - xh) + c) * ROWS, ROWS, 32)]
    weight_on = send(cross_weight, cross_weight, cross_ss.at[3], cross_rs.at[3], pair)
    weight_on.start()

    def place(core, column, slot):
        first = pl.multiple_of(core * 512 + column * NQ * PIECE, 128)
        for qq in range(NQ):
            piece = dweights[pl.ds(pl.multiple_of(first + qq * PIECE, 32), PIECE), :].astype(F32)
            for b in range(NB):
                spread[pl.ds((slot * NZ + NQ * b + qq) * 8, 8), :] = piece[b * 8 : (b + 1) * 8]
        to = dense_rows(column, core)
        for s in range(8):
            row = spread[pl.ds(slot * NZ * 8 + s, NZ, stride=8), :]
            dweight_out[to, s * 128 : (s + 1) * 128] = row.astype(BF16)

    order = (3, 1, 2, 0)
    backs = []
    for n in order:
        dx = (NX - DX[n]) % NX
        for k, (ddx, dz) in enumerate(NEAR):
            if ddx == dx:
                to_gather[k].wait_recv()
        group = dweights.at[at(c * 512 + columns[n] * NQ * PIECE, NQ * PIECE, 128)]
        back = send(group, group, back_send.at[n], back_recv.at[n], pair)
        back.start()
        backs.append(back)
        place(c, columns[n], n)
    for copy in to_gather:
        copy.wait_send()
    weight_pair.wait_recv()
    weight_on.wait()
    for n, back in zip(order, backs):
        back.wait_recv()
        place(1 - c, columns[n], 4 + n)
    for back in backs:
        back.wait_send()


def store(*refs):
    sources, outs, sem = refs[:8], refs[8:16], refs[16]
    copies = [pltpu.make_async_copy(s, o, sem.at[i]) for i, (s, o) in enumerate(zip(sources, outs))]
    for copy in copies:
        copy.start()
    for copy in copies:
        copy.wait()


def shards(
    expert_partials,
    token_counts,
    expert_master,
    expert_moment,
    expert_second,
    dense_partials,
    dense_master,
    dense_moment,
    dense_second,
):
    hbm = pl.BlockSpec(memory_space=pltpu.HBM)
    vmem = pl.BlockSpec(memory_space=pltpu.VMEM)
    dma = pltpu.SemaphoreType.DMA
    shapes = [
        ((4 * ROWS, COLS), BF16),
        ((ROWS, COLS), F32),
        ((ROWS, COLS), F32),
        ((ROWS, COLS), F32),
        ((128, 1024), BF16),
        ((8, 128), F32),
        ((8, 128), F32),
        ((8, 128), F32),
    ]
    n = len(NEAR)
    results = pl.pallas_call(
        exchange,
        out_shape=[pltpu.VMEM(s, d) for s, d in shapes],
        in_specs=[hbm] * 9,
        out_specs=[vmem] * 8,
        scratch_shapes=[
            pltpu.SMEM((1, 4), jnp.int32),
            pltpu.VMEM((4 * ROWS, COLS), BF16),
            pltpu.VMEM((3, ROWS, COLS), F32),
            pltpu.VMEM((2 * ROWS, COLS), BF16),
            pltpu.VMEM((2 * ROWS, COLS), BF16),
            pltpu.VMEM((ROWS, COLS), BF16),
            pltpu.VMEM((ROWS, COLS), BF16),
            pltpu.VMEM((64, 1024), BF16),
            pltpu.VMEM((64, 1024), BF16),
            pltpu.VMEM((64, 1024), BF16),
            pltpu.VMEM((512, 128), F32),
            pltpu.VMEM((512, 128), BF16),
            pltpu.VMEM((n * PIECE, 128), BF16),
            pltpu.VMEM((NB * PIECE, 128), BF16),
            pltpu.VMEM((NB * 24, 128), F32),
            pltpu.VMEM((NB * 24, 128), F32),
            pltpu.VMEM((1024, 128), BF16),
            pltpu.VMEM((1024, 128), F32),
            dma((19,)),
            dma((6,)),
            dma((6,)),
            dma((n,)),
            dma((n,)),
            dma((6,)),
            dma((6,)),
            dma((4,)),
            dma((4,)),
            dma((n,)),
            dma((n,)),
            dma((4,)),
            dma((4,)),
            pltpu.SemaphoreType.REGULAR,
            pltpu.SemaphoreType.REGULAR,
            pltpu.SemaphoreType.REGULAR,
        ],
        compiler_params=pltpu.CompilerParams(
            collective_id=0, has_side_effects=True, vmem_limit_bytes=56 * 2**20
        ),
        name="exchange",
    )(
        expert_partials.reshape(4 * ROWS, COLS),
        token_counts,
        expert_master,
        expert_moment,
        expert_second,
        dense_partials.reshape(128, 1024),
        dense_master.reshape(8, 128),
        dense_moment.reshape(8, 128),
        dense_second.reshape(8, 128),
    )
    outs = pl.pallas_call(
        store,
        out_shape=[jax.ShapeDtypeStruct(s, d) for s, d in shapes],
        in_specs=[vmem] * 8,
        out_specs=[hbm] * 8,
        scratch_shapes=[dma((8,))],
        compiler_params=pltpu.CompilerParams(vmem_limit_bytes=8 * 2**20),
        name="store",
    )(*results)
    outs = list(outs)
    outs[4] = outs[4].reshape(128, 1, 1024)
    for i in (5, 6, 7):
        outs[i] = outs[i].reshape(1024)
    return tuple(outs)


def solution(mesh):
    return jax.shard_map(
        shards,
        mesh=mesh,
        in_specs=(
            P("dp", "expert", "tensor"),
            P("dp", None),
            P(("expert", "dp"), "tensor"),
            P(("expert", "dp"), "tensor"),
            P(("expert", "dp"), "tensor"),
            P(("dp", "expert"), None, "tensor", None),
            P(("dp", "expert", "tensor")),
            P(("dp", "expert", "tensor")),
            P(("dp", "expert", "tensor")),
        ),
        out_specs=(
            P("expert", "tensor"),
            P(("expert", "dp"), "tensor"),
            P(("expert", "dp"), "tensor"),
            P(("expert", "dp"), "tensor"),
            P(None, "tensor", None),
            P(("dp", "expert", "tensor")),
            P(("dp", "expert", "tensor")),
            P(("dp", "expert", "tensor")),
        ),
        check_vma=False,
    )
```

```python
import functools

import jax
import jax.numpy as jnp
from jax import lax
from jax.experimental import pallas as pl
from jax.experimental.pallas import tpu as pltpu
from jax.sharding import PartitionSpec as P

MESH = pl.DeviceIdType.MESH
F32 = jnp.float32
BF16 = jnp.bfloat16

beta_one = 0.9
beta_two = 0.95
epsilon = 1e-08
learn_rate = 0.001
weight_decay = 0.1
bias_one = 1.0 - 0.9**10
bias_two = 1.0 - 0.95**10

NX, NZ, NQ = 4, 16, 4
NB = NZ // NQ
ROWS = 224
COLS = 256
PER_EXPERT = 8
PIECE = NB * 8
NEAR = (
    (1, 2), (3, 2), (0, 3), (0, -3),
    (2, 0), (1, 1), (3, 1), (1, -1), (3, -1), (0, 2), (0, -2),
    (1, 0), (3, 0), (0, 1), (0, -1),
)
FIRST = 4


def adam_update(weight, moment, second, gradient):
    moment_new = beta_one * moment + (1.0 - beta_one) * gradient
    second_new = beta_two * second + (1.0 - beta_two) * gradient * gradient
    ratio = moment_new / bias_one / (jnp.sqrt(second_new / bias_two) + epsilon)
    weight_new = weight - learn_rate * (ratio + weight_decay * weight)
    return (weight_new, moment_new, second_new)


def at(offset, size, unit):
    return pl.ds(pl.multiple_of(offset, unit), size)


def exchange(
    partials, counts, master, moment, second, dense, dmaster, dmoment, dsecond,
    weight_out, master_out, moment_out, second_out, dweight_out, dmaster_out, dmoment_out, dsecond_out,
    counts_s, blocks, states, scaled, pair_in, cross_send, cross_in,
    dense_own, dense_out, dense_in, tiles, pieces, near_in, far_buf, dstates, dnew, dweights, spread,
    load_sem, pair_sem, near_sem, far_sem, cross_sem, gather_sem, back_sem, known, pair_in_kernel, all_in_kernel,
):
    dp, ex = lax.axis_index("dp"), lax.axis_index("expert")
    xh, c = dp // 2, dp % 2
    xl, z = ex // NZ, ex % NZ
    x = 2 * xh + xl
    zb, q = z // NQ, z % NQ
    xc = (x + 2 * zb) % NX
    sign = 1 - 2 * c

    def device(x, z, c):
        return {"dp": ((x % NX) // 2) * 2 + c, "expert": (x % 2) * NZ + z % NZ}

    def slot(xc, q):
        return (xc % 2) * 8 + (xc // 2) * NQ + q

    def class_of(x, z):
        return slot((x + 2 * (z // NQ)) % NX, z % NQ)

    mine = class_of(x, z)

    def along(dz):
        return (z + sign * dz + NZ) % NZ

    pair = device(x, z, 1 - c)
    cross = device(x + 2, z, c)
    near = [device(x + dx, along(dz), c) for dx, dz in NEAR]
    near_back = [device(x + NX - dx, along(-dz), 1) for dx, dz in NEAR]
    far = [device(x + 2 * d, z + NQ * d, c) for d in range(1, NB)]

    def send(src, dst, ss, rs, to):
        return pltpu.make_async_remote_copy(
            src_ref=src, dst_ref=dst, send_sem=ss, recv_sem=rs, device_id=to, device_id_type=MESH
        )

    def wait_for(ref, sem):
        pltpu.make_async_copy(ref, ref, sem).wait()

    def dense_rows(column, core):
        return at(((column // 2) * 2 + core) * 32 + (column % 2) * NZ, NZ, 16)

    def dense_half(core, target, sem):
        return [
            pltpu.make_async_copy(
                dense.at[at((2 * h + core) * 32, 32, 32)], target.at[pl.ds(h * 32, 32)], load_sem.at[sem]
            )
            for h in range(2)
        ]

    own_states = dstates.at[at(zb * 24, 24, 8)]
    loads = dense_half(1 - c, dense_out, 0) + dense_half(c, dense_own, 1)
    loads += [
        pltpu.make_async_copy(counts, counts_s, load_sem.at[2]),
        pltpu.make_async_copy(partials, blocks, load_sem.at[3]),
    ]
    loads += [
        pltpu.make_async_copy(ref, dstates.at[at(zb * 24 + 8 * i, 8, 8)], load_sem.at[4])
        for i, ref in enumerate((dmaster, dmoment, dsecond))
    ]
    loads += [
        pltpu.make_async_copy(ref, states.at[i], load_sem.at[5]) for i, ref in enumerate((master, moment, second))
    ]
    for copy in loads[:2]:
        copy.start()

    barrier = pltpu.get_barrier_semaphore()

    @pl.when(c == 1)
    def _():
        pl.semaphore_signal(barrier, inc=1, device_id=pair, device_id_type=MESH)

    greeted = near_back + [device(x, z + NQ, 1), device(x, z + NZ - NQ, 1)]
    for other in greeted:
        pl.semaphore_signal(barrier, inc=1, device_id=other, device_id_type=MESH)

    for copy in loads[2:]:
        copy.start()

    @pl.when(c == 0)
    def _():
        pl.semaphore_wait(barrier, 1)
        pl.semaphore_signal(pair_in_kernel, inc=1, device_id=pair, device_id_type=MESH)

    @pl.when(c == 1)
    def _():
        pl.semaphore_wait(pair_in_kernel, 1)

    wait_for(dense_out, load_sem.at[0])
    dense_pair = send(dense_out, dense_in, pair_sem.at[0], pair_sem.at[1], pair)
    dense_pair.start()

    loads[4].wait()
    count = counts_s[0, ex // PER_EXPERT].astype(F32)
    inverse = 1.0 / jnp.full((1, COLS), count, F32)
    loads[5].wait()

    def scale(block, start):
        rows = pl.ds(pl.multiple_of(block * ROWS + start, 32), 32)
        return (blocks[rows].astype(F32) * inverse).astype(BF16)

    for h in range(2):
        block = 2 * (xh if h == 0 else 1 - xh) + 1 - c

        def scale_step(i, carry):
            scaled[pl.ds(pl.multiple_of(h * ROWS + i * 32, 32), 32)] = scale(block, i * 32)
            return carry

        lax.fori_loop(0, ROWS // 32, scale_step, 0)
    block_pair = send(scaled, pair_in, pair_sem.at[2], pair_sem.at[3], pair)
    block_pair.start()

    def sum_column(n):
        rows = pl.ds(n * NZ, NZ)
        total = dense_own[rows].astype(F32) + dense_in[rows].astype(F32)
        for s in range(8):
            tiles[pl.ds(n * NZ * 8 + s, NZ, stride=8), :] = total[:, s * 128 : (s + 1) * 128]

    wait_for(dense_own, load_sem.at[1])
    dense_pair.wait_recv()
    for n in range(NX):
        sum_column(n)
    for xx in range(NX):
        for qq in range(NQ):
            for half in range(NB // 2):
                two = [((xx + 2 * b) % NX * NZ + NQ * b + qq) * 8 for b in (2 * half, 2 * half + 1)]
                two = jnp.concatenate([tiles[pl.ds(first, 8), :] for first in two], axis=0)
                pieces[pl.ds(slot(xx, qq) * PIECE + half * 16, 16), :] = two.astype(BF16)

    @pl.when(c == 1)
    def _():
        pl.semaphore_wait(barrier, 2 * len(greeted))
        pl.semaphore_signal(all_in_kernel, inc=1, device_id=pair, device_id_type=MESH)

    @pl.when(c == 0)
    def _():
        pl.semaphore_wait(all_in_kernel, 1)

    to_near = [
        send(
            pieces.at[at(class_of(x + dx, along(dz)) * PIECE, PIECE, 32)],
            near_in.at[pl.ds(k * PIECE, PIECE)],
            near_sem.at[0], near_sem.at[1 if k < FIRST else 2], near[k],
        )
        for k, (dx, dz) in enumerate(NEAR)
    ]
    for copy in to_near:
        copy.start()

    for step in (NQ, NZ - NQ):
        pl.semaphore_signal(known, inc=1, device_id=device(x, z + step, c), device_id_type=MESH)

    block_pair.wait_recv()

    def cross_step(i, carry):
        off = pl.multiple_of(i * 32, 32)
        own = scale(2 * (1 - xh) + c, off)
        other = pair_in[pl.ds(pl.multiple_of(ROWS + off, 32), 32)]
        cross_send[pl.ds(off, 32)] = (own.astype(F32) + other.astype(F32)).astype(BF16)
        return carry

    lax.fori_loop(0, ROWS // 32, cross_step, 0)
    wait_for(own_states, load_sem.at[4])
    pl.semaphore_wait(known, 2)
    to_states = [send(own_states, own_states, far_sem.at[0], far_sem.at[1], far[d]) for d in (1, 0, 2)]
    for copy in to_states:
        copy.start()
    to_cross = send(cross_send, cross_in, cross_sem.at[0], cross_sem.at[1], cross)

    total = [tiles[at(((xc + 2 * b) % NX * NZ + NQ * b + q) * 8, 8, 8), :] for b in range(NB)]
    total = jnp.concatenate(total, axis=0)
    wait_for(near_in.at[pl.ds(FIRST * PIECE, (len(NEAR) - FIRST) * PIECE)], near_sem.at[2])
    to_cross.start()
    for k in range(FIRST, len(NEAR)):
        total = total + near_in[pl.ds(k * PIECE, PIECE), :].astype(F32)
    wait_for(near_in.at[pl.ds(0, FIRST * PIECE)], near_sem.at[1])
    for k in range(FIRST):
        total = total + near_in[pl.ds(k * PIECE, PIECE), :].astype(F32)
    far_own = far_buf.at[at(zb * PIECE, PIECE, 32)]
    far_own[...] = total.astype(BF16)
    to_far = [send(far_own, far_own, far_sem.at[2], far_sem.at[3], far[d]) for d in (1, 0, 2)]
    for copy in to_far:
        copy.start()

    wait_for(states, load_sem.at[5])
    dense_pair.wait_send()
    block_pair.wait_send()
    wait_for(near_in, near_sem.at[0])
    to_cross.wait_recv()

    def update_step(i, carry):
        off = pl.multiple_of(i * 32, 32)
        rows = pl.ds(off, 32)
        own = scale(dp, off)
        gradient = own.astype(F32) + pair_in[rows].astype(F32) + cross_in[rows].astype(F32)
        new, moment_new, second_new = adam_update(states[0, rows], states[1, rows], states[2, rows], gradient)
        master_out[rows] = new
        moment_out[rows] = moment_new
        second_out[rows] = second_new
        weight_out[pl.ds(pl.multiple_of(dp * ROWS + off, 32), 32)] = new.astype(BF16)
        return carry

    lax.fori_loop(0, ROWS // 32, update_step, 0)
    own_weight = weight_out.at[at(dp * ROWS, ROWS, 32)]
    weight_cross = send(own_weight, own_weight, cross_sem.at[2], cross_sem.at[3], cross)
    weight_cross.start()
    weight_pair = send(own_weight, own_weight, cross_sem.at[2], cross_sem.at[4], pair)
    weight_pair.start()

    wait_for(dstates.at[pl.ds(0, 72)], far_sem.at[0])
    wait_for(dstates.at[pl.ds(0, 72)], far_sem.at[1])
    to_cross.wait_send()
    wait_for(far_buf.at[pl.ds(0, 3 * PIECE)], far_sem.at[3])
    dense_sum = jnp.zeros((PIECE, 128), F32)
    for b in range(NB):
        dense_sum = dense_sum + far_buf[pl.ds(b * PIECE, PIECE), :].astype(F32)
    news = []
    for b in range(NB):
        old = [dstates[pl.ds(b * 24 + 8 * i, 8), :] for i in range(3)]
        new = adam_update(*old, dense_sum[b * 8 : (b + 1) * 8])
        for i in range(3):
            dnew[pl.ds(b * 24 + 8 * i, 8), :] = new[i]
        news.append(new[0])
    own_piece = dweights.at[at(c * 512 + mine * PIECE, PIECE, 32)]
    own_piece[...] = jnp.concatenate(news, axis=0).astype(BF16)
    to_gather = [
        send(own_piece, own_piece, gather_sem.at[0], gather_sem.at[1 + xc], other) for other in near
    ]
    for copy in to_gather:
        copy.start()
    for i, ref in enumerate((dmaster_out, dmoment_out, dsecond_out)):
        ref[...] = dnew[at(zb * 24 + 8 * i, 8, 8), :]
    wait_for(far_buf.at[pl.ds(0, 3 * PIECE)], far_sem.at[2])

    weight_cross.wait_recv()
    cross_weight = weight_out.at[at((2 * (1 - xh) + c) * ROWS, ROWS, 32)]
    weight_on = send(cross_weight, cross_weight, cross_sem.at[2], cross_sem.at[4], pair)
    weight_on.start()

    def place(core, parity):
        first = core * 512 + parity * 8 * PIECE
        for qq in range(NQ):
            even = dweights[at(first + qq * PIECE, PIECE, 32), :].astype(F32)
            odd = dweights[at(first + (NQ + qq) * PIECE, PIECE, 32), :].astype(F32)
            for b in range(NB):
                for n, piece in enumerate((even, odd) if b % 2 == 0 else (odd, even)):
                    spread[pl.ds((n * NZ + NQ * b + qq) * 8, 8), :] = piece[b * 8 : (b + 1) * 8]
        for n in range(2):
            to = at((2 * n + core) * 32 + parity * NZ, NZ, 16)
            for s in range(8):
                row = spread[pl.ds(n * NZ * 8 + s, NZ, stride=8), :]
                dweight_out[to, s * 128 : (s + 1) * 128] = row.astype(BF16)

    for step in (0, 2, 1, 3):
        xs = (xc + step) % NX
        pieces_in = NQ - 1 if step == 0 else NQ
        wait_for(dweights.at[pl.ds(0, pieces_in * PIECE)], gather_sem.at[1 + xs])
        group = dweights.at[at(c * 512 + slot(xs, 0) * PIECE, NQ * PIECE, 128)]
        send(group, group, back_sem.at[0], back_sem.at[1 + step % 2], pair).start()
        if step >= 2:
            place(c, (x + step) % 2)
    wait_for(near_in, gather_sem.at[0])
    wait_for(weight_out.at[pl.ds(0, 3 * ROWS)], cross_sem.at[2])
    wait_for(weight_out.at[pl.ds(0, 2 * ROWS)], cross_sem.at[4])
    for step in range(2):
        wait_for(dweights.at[pl.ds(0, 2 * NQ * PIECE)], back_sem.at[1 + step])
        place(1 - c, (x + step) % 2)
    wait_for(dweights.at[pl.ds(0, 4 * NQ * PIECE)], back_sem.at[0])


def store(*refs):
    sources, outs, sem = refs[:8], refs[8:16], refs[16]
    copies = [pltpu.make_async_copy(s, o, sem.at[i]) for i, (s, o) in enumerate(zip(sources, outs))]
    for copy in copies:
        copy.start()
    for copy in copies:
        copy.wait()


def shards(
    expert_partials,
    token_counts,
    expert_master,
    expert_moment,
    expert_second,
    dense_partials,
    dense_master,
    dense_moment,
    dense_second,
):
    hbm = pl.BlockSpec(memory_space=pltpu.HBM)
    vmem = pl.BlockSpec(memory_space=pltpu.VMEM)
    dma = pltpu.SemaphoreType.DMA
    shapes = [
        ((4 * ROWS, COLS), BF16),
        ((ROWS, COLS), F32),
        ((ROWS, COLS), F32),
        ((ROWS, COLS), F32),
        ((128, 1024), BF16),
        ((8, 128), F32),
        ((8, 128), F32),
        ((8, 128), F32),
    ]
    results = pl.pallas_call(
        exchange,
        out_shape=[pltpu.VMEM(s, d) for s, d in shapes],
        in_specs=[hbm] * 9,
        out_specs=[vmem] * 8,
        scratch_shapes=[
            pltpu.SMEM((1, 4), jnp.int32),
            pltpu.VMEM((4 * ROWS, COLS), BF16),
            pltpu.VMEM((3, ROWS, COLS), F32),
            pltpu.VMEM((2 * ROWS, COLS), BF16),
            pltpu.VMEM((2 * ROWS, COLS), BF16),
            pltpu.VMEM((ROWS, COLS), BF16),
            pltpu.VMEM((ROWS, COLS), BF16),
            pltpu.VMEM((64, 1024), BF16),
            pltpu.VMEM((64, 1024), BF16),
            pltpu.VMEM((64, 1024), BF16),
            pltpu.VMEM((512, 128), F32),
            pltpu.VMEM((512, 128), BF16),
            pltpu.VMEM((len(NEAR) * PIECE, 128), BF16),
            pltpu.VMEM((NB * PIECE, 128), BF16),
            pltpu.VMEM((NB * 24, 128), F32),
            pltpu.VMEM((NB * 24, 128), F32),
            pltpu.VMEM((1024, 128), BF16),
            pltpu.VMEM((1024, 128), F32),
            dma((6,)),
            dma((4,)),
            dma((3,)),
            dma((4,)),
            dma((5,)),
            dma((5,)),
            dma((3,)),
            pltpu.SemaphoreType.REGULAR,
            pltpu.SemaphoreType.REGULAR,
            pltpu.SemaphoreType.REGULAR,
        ],
        compiler_params=pltpu.CompilerParams(
            collective_id=0, has_side_effects=True, vmem_limit_bytes=56 * 2**20
        ),
        name="exchange",
    )(
        expert_partials.reshape(4 * ROWS, COLS),
        token_counts,
        expert_master,
        expert_moment,
        expert_second,
        dense_partials.reshape(128, 1024),
        dense_master.reshape(8, 128),
        dense_moment.reshape(8, 128),
        dense_second.reshape(8, 128),
    )
    outs = pl.pallas_call(
        store,
        out_shape=[jax.ShapeDtypeStruct(s, d) for s, d in shapes],
        in_specs=[vmem] * 8,
        out_specs=[hbm] * 8,
        scratch_shapes=[dma((8,))],
        compiler_params=pltpu.CompilerParams(vmem_limit_bytes=8 * 2**20),
        name="store",
    )(*results)
    outs = list(outs)
    outs[4] = outs[4].reshape(128, 1, 1024)
    for i in (5, 6, 7):
        outs[i] = outs[i].reshape(1024)
    return tuple(outs)


def solution(mesh):
    return jax.shard_map(
        shards,
        mesh=mesh,
        in_specs=(
            P("dp", "expert", "tensor"),
            P("dp", None),
            P(("expert", "dp"), "tensor"),
            P(("expert", "dp"), "tensor"),
            P(("expert", "dp"), "tensor"),
            P(("dp", "expert"), None, "tensor", None),
            P(("dp", "expert", "tensor")),
            P(("dp", "expert", "tensor")),
            P(("dp", "expert", "tensor")),
        ),
        out_specs=(
            P("expert", "tensor"),
            P(("expert", "dp"), "tensor"),
            P(("expert", "dp"), "tensor"),
            P(("expert", "dp"), "tensor"),
            P(None, "tensor", None),
            P(("dp", "expert", "tensor")),
            P(("dp", "expert", "tensor")),
            P(("dp", "expert", "tensor")),
        ),
        check_vma=False,
    )
```

```python
import functools

import jax
import jax.numpy as jnp
from jax import lax
from jax.experimental import pallas as pl
from jax.experimental.pallas import tpu as pltpu
from jax.sharding import PartitionSpec as P

MESH = pl.DeviceIdType.MESH
F32 = jnp.float32
BF16 = jnp.bfloat16

beta_one = 0.9
beta_two = 0.95
epsilon = 1e-08
learn_rate = 0.001
weight_decay = 0.1
bias_one = 1.0 - 0.9**10
bias_two = 1.0 - 0.95**10

NX, NZ, NQ = 4, 16, 4
NB = NZ // NQ
ROWS = 224
COLS = 256
PER_EXPERT = 8
PIECE = NB * 8
DX = (2, 1, 3, 0)
DZ = (-2, 1, -1, 0)
GROUPS = ((0,), (1, 2), (3,))
FIRST = 4
NEAR = [(DX[n], dz) for group in GROUPS for dz in DZ for n in group if (DX[n], dz) != (0, 0)]


def adam_update(weight, moment, second, gradient):
    moment_new = beta_one * moment + (1.0 - beta_one) * gradient
    second_new = beta_two * second + (1.0 - beta_two) * gradient * gradient
    ratio = moment_new / bias_one / (jnp.sqrt(second_new / bias_two) + epsilon)
    weight_new = weight - learn_rate * (ratio + weight_decay * weight)
    return (weight_new, moment_new, second_new)


def at(offset, size, unit):
    return pl.ds(pl.multiple_of(offset, unit), size)


def exchange(
    partials, counts, master, moment, second, dense, dmaster, dmoment, dsecond,
    weight_out, master_out, moment_out, second_out, dweight_out, dmaster_out, dmoment_out, dsecond_out,
    counts_s, blocks, states, scaled, pair_in, cross_send, cross_in,
    dense_own, dense_out, dense_in, tiles, pieces, near_in, far_buf, dstates, dnew, dweights, spread,
    load_sem, pair_sem, near_sem, far_sem, cross_sem, gather_sem, back_sem, known, pair_in_kernel, all_in_kernel,
):
    dp, ex = lax.axis_index("dp"), lax.axis_index("expert")
    xh, c = dp // 2, dp % 2
    xl, z = ex // NZ, ex % NZ
    x = 2 * xh + xl
    zb, q = z // NQ, z % NQ
    sign = 1 - 2 * c

    def device(x, z, c):
        return {"dp": ((x % NX) // 2) * 2 + c, "expert": (x % 2) * NZ + z % NZ}

    def along(dz):
        return (z + sign * dz + NZ) % NZ

    pair = device(x, z, 1 - c)
    cross = device(x + 2, z, c)
    near = [device(x + dx, along(dz), c) for dx, dz in NEAR]
    near_back = [device(x + NX - dx, along(-dz), 1) for dx, dz in NEAR]
    far = [device(x, z + NQ * d, c) for d in range(1, NB)]

    def send(src, dst, ss, rs, to):
        return pltpu.make_async_remote_copy(
            src_ref=src, dst_ref=dst, send_sem=ss, recv_sem=rs, device_id=to, device_id_type=MESH
        )

    def wait_for(ref, sem):
        pltpu.make_async_copy(ref, ref, sem).wait()

    def dense_rows(column, core):
        return at(((column // 2) * 2 + core) * 32 + (column % 2) * NZ, NZ, 16)

    def dense_half(core, target, sem):
        return [
            pltpu.make_async_copy(
                dense.at[at((2 * h + core) * 32, 32, 32)], target.at[pl.ds(h * 32, 32)], load_sem.at[sem]
            )
            for h in range(2)
        ]

    own_states = dstates.at[at(zb * 24, 24, 8)]
    loads = dense_half(1 - c, dense_out, 0) + dense_half(c, dense_own, 1)
    loads += [
        pltpu.make_async_copy(counts, counts_s, load_sem.at[2]),
        pltpu.make_async_copy(partials, blocks, load_sem.at[3]),
    ]
    loads += [
        pltpu.make_async_copy(ref, dstates.at[at(zb * 24 + 8 * i, 8, 8)], load_sem.at[4])
        for i, ref in enumerate((dmaster, dmoment, dsecond))
    ]
    loads += [
        pltpu.make_async_copy(ref, states.at[i], load_sem.at[5]) for i, ref in enumerate((master, moment, second))
    ]
    for copy in loads[:2]:
        copy.start()

    barrier = pltpu.get_barrier_semaphore()

    @pl.when(c == 1)
    def _():
        pl.semaphore_signal(barrier, inc=1, device_id=pair, device_id_type=MESH)

    greeted = near_back + [device(x, z + NQ, 1), device(x, z + NZ - NQ, 1)]
    for other in greeted:
        pl.semaphore_signal(barrier, inc=1, device_id=other, device_id_type=MESH)

    for copy in loads[2:]:
        copy.start()

    @pl.when(c == 0)
    def _():
        pl.semaphore_wait(barrier, 1)
        pl.semaphore_signal(pair_in_kernel, inc=1, device_id=pair, device_id_type=MESH)

    @pl.when(c == 1)
    def _():
        pl.semaphore_wait(pair_in_kernel, 1)

    wait_for(dense_out, load_sem.at[0])
    dense_pair = send(dense_out, dense_in, pair_sem.at[0], pair_sem.at[1], pair)
    dense_pair.start()

    loads[4].wait()
    count = counts_s[0, ex // PER_EXPERT].astype(F32)
    inverse = 1.0 / jnp.full((1, COLS), count, F32)
    loads[5].wait()

    def scale(block, start):
        rows = pl.ds(pl.multiple_of(block * ROWS + start, 32), 32)
        return (blocks[rows].astype(F32) * inverse).astype(BF16)

    for h in range(2):
        block = 2 * (xh if h == 0 else 1 - xh) + 1 - c

        def scale_step(i, carry):
            scaled[pl.ds(pl.multiple_of(h * ROWS + i * 32, 32), 32)] = scale(block, i * 32)
            return carry

        lax.fori_loop(0, ROWS // 32, scale_step, 0)
    block_pair = send(scaled, pair_in, pair_sem.at[2], pair_sem.at[3], pair)
    block_pair.start()

    def sum_column(n):
        rows = pl.ds(n * NZ, NZ)
        total = dense_own[rows].astype(F32) + dense_in[rows].astype(F32)
        for s in range(8):
            tiles[pl.ds(n * NZ * 8 + s, NZ, stride=8), :] = total[:, s * 128 : (s + 1) * 128]
        for qq in range(NQ):
            for half in range(NB // 2):
                two = [tiles[pl.ds((n * NZ + NQ * (2 * half + k) + qq) * 8, 8), :] for k in range(2)]
                pieces[pl.ds((n * NQ + qq) * PIECE + half * 16, 16), :] = jnp.concatenate(two, axis=0).astype(BF16)

    wait_for(dense_own, load_sem.at[1])
    dense_pair.wait_recv()
    for n in range(NX):
        sum_column(n)

    @pl.when(c == 1)
    def _():
        pl.semaphore_wait(barrier, 2 * len(greeted))
        pl.semaphore_signal(all_in_kernel, inc=1, device_id=pair, device_id_type=MESH)

    @pl.when(c == 0)
    def _():
        pl.semaphore_wait(all_in_kernel, 1)

    to_near = [
        send(
            pieces.at[at(((x + dx) % NX * NQ + along(dz) % NQ) * PIECE, PIECE, 32)],
            near_in.at[pl.ds(k * PIECE, PIECE)],
            near_sem.at[0], near_sem.at[1 if k < FIRST else 2], near[k],
        )
        for k, (dx, dz) in enumerate(NEAR)
    ]
    for copy in to_near:
        copy.start()

    pl.semaphore_signal(known, inc=1, device_id=far[0], device_id_type=MESH)
    wait_for(own_states, load_sem.at[4])
    to_states = [send(own_states, own_states, far_sem.at[0], far_sem.at[1], far[d]) for d in range(NB - 1)]
    to_states[0].start()
    to_states[2].start()

    block_pair.wait_recv()

    def cross_step(i, carry):
        off = pl.multiple_of(i * 32, 32)
        own = scale(2 * (1 - xh) + c, off)
        other = pair_in[pl.ds(pl.multiple_of(ROWS + off, 32), 32)]
        cross_send[pl.ds(off, 32)] = (own.astype(F32) + other.astype(F32)).astype(BF16)
        return carry

    lax.fori_loop(0, ROWS // 32, cross_step, 0)
    pl.semaphore_wait(known, 1)
    to_states[1].start()
    to_cross = send(cross_send, cross_in, cross_sem.at[0], cross_sem.at[1], cross)

    total = [tiles[at((x * NZ + NQ * b + q) * 8, 8, 8), :] for b in range(NB)]
    total = jnp.concatenate(total, axis=0)
    wait_for(near_in.at[pl.ds(FIRST * PIECE, (len(NEAR) - FIRST) * PIECE)], near_sem.at[2])
    to_cross.start()
    for k in range(FIRST, len(NEAR)):
        total = total + near_in[pl.ds(k * PIECE, PIECE), :].astype(F32)
    wait_for(near_in.at[pl.ds(0, FIRST * PIECE)], near_sem.at[1])
    for k in range(FIRST):
        total = total + near_in[pl.ds(k * PIECE, PIECE), :].astype(F32)
    far_own = far_buf.at[at(zb * PIECE, PIECE, 32)]
    far_own[...] = total.astype(BF16)
    to_far = [send(far_own, far_own, far_sem.at[2], far_sem.at[3], far[d]) for d in (1, 0, 2)]
    for copy in to_far:
        copy.start()

    wait_for(states, load_sem.at[5])
    dense_pair.wait_send()
    block_pair.wait_send()
    wait_for(near_in, near_sem.at[0])
    to_cross.wait_recv()

    def update_step(i, carry):
        off = pl.multiple_of(i * 32, 32)
        rows = pl.ds(off, 32)
        own = scale(dp, off)
        gradient = own.astype(F32) + pair_in[rows].astype(F32) + cross_in[rows].astype(F32)
        new, moment_new, second_new = adam_update(states[0, rows], states[1, rows], states[2, rows], gradient)
        master_out[rows] = new
        moment_out[rows] = moment_new
        second_out[rows] = second_new
        weight_out[pl.ds(pl.multiple_of(dp * ROWS + off, 32), 32)] = new.astype(BF16)
        return carry

    lax.fori_loop(0, ROWS // 32, update_step, 0)
    own_weight = weight_out.at[at(dp * ROWS, ROWS, 32)]
    weight_cross = send(own_weight, own_weight, cross_sem.at[2], cross_sem.at[3], cross)
    weight_cross.start()
    weight_pair = send(own_weight, own_weight, cross_sem.at[2], cross_sem.at[4], pair)
    weight_pair.start()

    wait_for(dstates.at[pl.ds(0, 72)], far_sem.at[0])
    wait_for(dstates.at[pl.ds(0, 72)], far_sem.at[1])
    to_cross.wait_send()
    wait_for(far_buf.at[pl.ds(0, 3 * PIECE)], far_sem.at[3])
    dense_sum = jnp.zeros((PIECE, 128), F32)
    for b in range(NB):
        dense_sum = dense_sum + far_buf[pl.ds(b * PIECE, PIECE), :].astype(F32)
    news = []
    for b in range(NB):
        old = [dstates[pl.ds(b * 24 + 8 * i, 8), :] for i in range(3)]
        new = adam_update(*old, dense_sum[b * 8 : (b + 1) * 8])
        for i in range(3):
            dnew[pl.ds(b * 24 + 8 * i, 8), :] = new[i]
        news.append(new[0])
    own_piece = dweights.at[at(c * 512 + (x * NQ + q) * PIECE, PIECE, 32)]
    own_piece[...] = jnp.concatenate(news, axis=0).astype(BF16)
    to_gather = [
        send(own_piece, own_piece, gather_sem.at[0], gather_sem.at[1 + dx], near[k])
        for k, (dx, dz) in enumerate(NEAR)
    ]
    for copy in to_gather:
        copy.start()
    for i, ref in enumerate((dmaster_out, dmoment_out, dsecond_out)):
        ref[...] = dnew[at(zb * 24 + 8 * i, 8, 8), :]
    wait_for(far_buf.at[pl.ds(0, 3 * PIECE)], far_sem.at[2])

    weight_cross.wait_recv()
    cross_weight = weight_out.at[at((2 * (1 - xh) + c) * ROWS, ROWS, 32)]
    weight_on = send(cross_weight, cross_weight, cross_sem.at[2], cross_sem.at[4], pair)
    weight_on.start()

    def place(core, column, slot):
        first = pl.multiple_of(core * 512 + column * NQ * PIECE, 128)
        for qq in range(NQ):
            piece = dweights[pl.ds(pl.multiple_of(first + qq * PIECE, 32), PIECE), :].astype(F32)
            for b in range(NB):
                spread[pl.ds((slot * NZ + NQ * b + qq) * 8, 8), :] = piece[b * 8 : (b + 1) * 8]
        to = dense_rows(column, core)
        for s in range(8):
            row = spread[pl.ds(slot * NZ * 8 + s, NZ, stride=8), :]
            dweight_out[to, s * 128 : (s + 1) * 128] = row.astype(BF16)

    order = (0, 1, 3, 2)
    for dx in order:
        column = (x + NX - dx) % NX
        pieces_in = NQ - 1 if dx == 0 else NQ
        wait_for(dweights.at[pl.ds(0, pieces_in * PIECE)], gather_sem.at[1 + dx])
        group = dweights.at[at(c * 512 + column * NQ * PIECE, NQ * PIECE, 128)]
        send(group, group, back_sem.at[0], back_sem.at[1 if dx != 2 else 2], pair).start()
        place(c, column, dx)
    wait_for(near_in, gather_sem.at[0])
    wait_for(weight_out.at[pl.ds(0, 3 * ROWS)], cross_sem.at[2])
    wait_for(weight_out.at[pl.ds(0, 2 * ROWS)], cross_sem.at[4])
    wait_for(dweights.at[pl.ds(0, 3 * NQ * PIECE)], back_sem.at[1])
    for dx in order[:3]:
        place(1 - c, (x + NX - dx) % NX, 4 + dx)
    wait_for(dweights.at[pl.ds(0, NQ * PIECE)], back_sem.at[2])
    place(1 - c, (x + 2) % NX, 6)
    wait_for(dweights.at[pl.ds(0, 4 * NQ * PIECE)], back_sem.at[0])


def store(*refs):
    sources, outs, sem = refs[:8], refs[8:16], refs[16]
    copies = [pltpu.make_async_copy(s, o, sem.at[i]) for i, (s, o) in enumerate(zip(sources, outs))]
    for copy in copies:
        copy.start()
    for copy in copies:
        copy.wait()


def shards(
    expert_partials,
    token_counts,
    expert_master,
    expert_moment,
    expert_second,
    dense_partials,
    dense_master,
    dense_moment,
    dense_second,
):
    hbm = pl.BlockSpec(memory_space=pltpu.HBM)
    vmem = pl.BlockSpec(memory_space=pltpu.VMEM)
    dma = pltpu.SemaphoreType.DMA
    shapes = [
        ((4 * ROWS, COLS), BF16),
        ((ROWS, COLS), F32),
        ((ROWS, COLS), F32),
        ((ROWS, COLS), F32),
        ((128, 1024), BF16),
        ((8, 128), F32),
        ((8, 128), F32),
        ((8, 128), F32),
    ]
    results = pl.pallas_call(
        exchange,
        out_shape=[pltpu.VMEM(s, d) for s, d in shapes],
        in_specs=[hbm] * 9,
        out_specs=[vmem] * 8,
        scratch_shapes=[
            pltpu.SMEM((1, 4), jnp.int32),
            pltpu.VMEM((4 * ROWS, COLS), BF16),
            pltpu.VMEM((3, ROWS, COLS), F32),
            pltpu.VMEM((2 * ROWS, COLS), BF16),
            pltpu.VMEM((2 * ROWS, COLS), BF16),
            pltpu.VMEM((ROWS, COLS), BF16),
            pltpu.VMEM((ROWS, COLS), BF16),
            pltpu.VMEM((64, 1024), BF16),
            pltpu.VMEM((64, 1024), BF16),
            pltpu.VMEM((64, 1024), BF16),
            pltpu.VMEM((512, 128), F32),
            pltpu.VMEM((512, 128), BF16),
            pltpu.VMEM((len(NEAR) * PIECE, 128), BF16),
            pltpu.VMEM((NB * PIECE, 128), BF16),
            pltpu.VMEM((NB * 24, 128), F32),
            pltpu.VMEM((NB * 24, 128), F32),
            pltpu.VMEM((1024, 128), BF16),
            pltpu.VMEM((1024, 128), F32),
            dma((6,)),
            dma((4,)),
            dma((3,)),
            dma((4,)),
            dma((5,)),
            dma((5,)),
            dma((3,)),
            pltpu.SemaphoreType.REGULAR,
            pltpu.SemaphoreType.REGULAR,
            pltpu.SemaphoreType.REGULAR,
        ],
        compiler_params=pltpu.CompilerParams(
            collective_id=0, has_side_effects=True, vmem_limit_bytes=56 * 2**20
        ),
        name="exchange",
    )(
        expert_partials.reshape(4 * ROWS, COLS),
        token_counts,
        expert_master,
        expert_moment,
        expert_second,
        dense_partials.reshape(128, 1024),
        dense_master.reshape(8, 128),
        dense_moment.reshape(8, 128),
        dense_second.reshape(8, 128),
    )
    outs = pl.pallas_call(
        store,
        out_shape=[jax.ShapeDtypeStruct(s, d) for s, d in shapes],
        in_specs=[vmem] * 8,
        out_specs=[hbm] * 8,
        scratch_shapes=[dma((8,))],
        compiler_params=pltpu.CompilerParams(vmem_limit_bytes=8 * 2**20),
        name="store",
    )(*results)
    outs = list(outs)
    outs[4] = outs[4].reshape(128, 1, 1024)
    for i in (5, 6, 7):
        outs[i] = outs[i].reshape(1024)
    return tuple(outs)


def solution(mesh):
    return jax.shard_map(
        shards,
        mesh=mesh,
        in_specs=(
            P("dp", "expert", "tensor"),
            P("dp", None),
            P(("expert", "dp"), "tensor"),
            P(("expert", "dp"), "tensor"),
            P(("expert", "dp"), "tensor"),
            P(("dp", "expert"), None, "tensor", None),
            P(("dp", "expert", "tensor")),
            P(("dp", "expert", "tensor")),
            P(("dp", "expert", "tensor")),
        ),
        out_specs=(
            P("expert", "tensor"),
            P(("expert", "dp"), "tensor"),
            P(("expert", "dp"), "tensor"),
            P(("expert", "dp"), "tensor"),
            P(None, "tensor", None),
            P(("dp", "expert", "tensor")),
            P(("dp", "expert", "tensor")),
            P(("dp", "expert", "tensor")),
        ),
        check_vma=False,
    )
```

```python
import functools

import jax
import jax.numpy as jnp
from jax import lax
from jax.experimental import pallas as pl
from jax.experimental.pallas import tpu as pltpu
from jax.sharding import PartitionSpec as P

MESH = pl.DeviceIdType.MESH
F32 = jnp.float32
BF16 = jnp.bfloat16

beta_one = 0.9
beta_two = 0.95
epsilon = 1e-08
learn_rate = 0.001
weight_decay = 0.1
bias_one = 1.0 - 0.9**10
bias_two = 1.0 - 0.95**10

NX, NZ, NQ = 4, 16, 4
NB = NZ // NQ
ROWS = 224
COLS = 256
PER_EXPERT = 8
PIECE = NB * 8
DX = (2, 1, 3, 0)
DZ = (-2, 1, -1, 0)
GROUPS = ((0,), (1, 2), (3,))
FIRST = 4
NEAR = [(DX[n], dz) for group in GROUPS for dz in DZ for n in group if (DX[n], dz) != (0, 0)]


def adam_update(weight, moment, second, gradient):
    moment_new = beta_one * moment + (1.0 - beta_one) * gradient
    second_new = beta_two * second + (1.0 - beta_two) * gradient * gradient
    ratio = moment_new / bias_one / (jnp.sqrt(second_new / bias_two) + epsilon)
    weight_new = weight - learn_rate * (ratio + weight_decay * weight)
    return (weight_new, moment_new, second_new)


def at(offset, size, unit):
    return pl.ds(pl.multiple_of(offset, unit), size)


def exchange(
    partials, counts, master, moment, second, dense, dmaster, dmoment, dsecond,
    weight_out, master_out, moment_out, second_out, dweight_out, dmaster_out, dmoment_out, dsecond_out,
    counts_s, blocks, states, scaled, pair_in, cross_send, cross_in,
    dense_own, dense_out, dense_in, tiles, pieces, near_in, far_buf, dstates, dnew, dweights, spread,
    load_sem, pair_sem, near_sem, far_sem, cross_sem, gather_sem, back_sem, known, pair_in_kernel, all_in_kernel,
):
    dp, ex = lax.axis_index("dp"), lax.axis_index("expert")
    xh, c = dp // 2, dp % 2
    xl, z = ex // NZ, ex % NZ
    x = 2 * xh + xl
    zb, q = z // NQ, z % NQ
    sign = 2 * c - 1

    def device(x, z, c):
        return {"dp": ((x % NX) // 2) * 2 + c, "expert": (x % 2) * NZ + z % NZ}

    def along(dz):
        return (z + sign * dz + NZ) % NZ

    pair = device(x, z, 1 - c)
    cross = device(x + 2, z, c)
    near = [device(x + dx, along(dz), c) for dx, dz in NEAR]
    near_back = [device(x + NX - dx, along(-dz), 1) for dx, dz in NEAR]
    far = [device(x, z + NQ * d, c) for d in range(1, NB)]

    def send(src, dst, ss, rs, to):
        return pltpu.make_async_remote_copy(
            src_ref=src, dst_ref=dst, send_sem=ss, recv_sem=rs, device_id=to, device_id_type=MESH
        )

    def wait_for(ref, sem):
        pltpu.make_async_copy(ref, ref, sem).wait()

    def dense_rows(column, core):
        return at(((column // 2) * 2 + core) * 32 + (column % 2) * NZ, NZ, 16)

    def dense_half(core, target, sem):
        return [
            pltpu.make_async_copy(
                dense.at[at((2 * h + core) * 32, 32, 32)], target.at[pl.ds(h * 32, 32)], load_sem.at[sem]
            )
            for h in range(2)
        ]

    own_states = dstates.at[at(zb * 24, 24, 8)]
    loads = dense_half(1 - c, dense_out, 0) + dense_half(c, dense_own, 1)
    loads += [
        pltpu.make_async_copy(counts, counts_s, load_sem.at[2]),
        pltpu.make_async_copy(partials, blocks, load_sem.at[3]),
    ]
    loads += [
        pltpu.make_async_copy(ref, dstates.at[at(zb * 24 + 8 * i, 8, 8)], load_sem.at[4])
        for i, ref in enumerate((dmaster, dmoment, dsecond))
    ]
    loads += [
        pltpu.make_async_copy(ref, states.at[i], load_sem.at[5]) for i, ref in enumerate((master, moment, second))
    ]
    for copy in loads[:2]:
        copy.start()

    barrier = pltpu.get_barrier_semaphore()

    @pl.when(c == 1)
    def _():
        pl.semaphore_signal(barrier, inc=1, device_id=pair, device_id_type=MESH)

    greeted = near_back + [device(x, z + NQ, 1), device(x, z + NZ - NQ, 1)]
    for other in greeted:
        pl.semaphore_signal(barrier, inc=1, device_id=other, device_id_type=MESH)

    for copy in loads[2:]:
        copy.start()

    @pl.when(c == 0)
    def _():
        pl.semaphore_wait(barrier, 1)
        pl.semaphore_signal(pair_in_kernel, inc=1, device_id=pair, device_id_type=MESH)

    @pl.when(c == 1)
    def _():
        pl.semaphore_wait(pair_in_kernel, 1)

    wait_for(dense_out, load_sem.at[0])
    dense_pair = send(dense_out, dense_in, pair_sem.at[0], pair_sem.at[1], pair)
    dense_pair.start()

    loads[4].wait()
    count = counts_s[0, ex // PER_EXPERT].astype(F32)
    inverse = 1.0 / jnp.full((1, COLS), count, F32)
    loads[5].wait()

    def scale(block, start):
        rows = pl.ds(pl.multiple_of(block * ROWS + start, 32), 32)
        return (blocks[rows].astype(F32) * inverse).astype(BF16)

    for h in range(2):
        block = 2 * (xh if h == 0 else 1 - xh) + 1 - c

        def scale_step(i, carry):
            scaled[pl.ds(pl.multiple_of(h * ROWS + i * 32, 32), 32)] = scale(block, i * 32)
            return carry

        lax.fori_loop(0, ROWS // 32, scale_step, 0)
    block_pair = send(scaled, pair_in, pair_sem.at[2], pair_sem.at[3], pair)
    block_pair.start()

    def sum_column(n):
        rows = pl.ds(n * NZ, NZ)
        total = dense_own[rows].astype(F32) + dense_in[rows].astype(F32)
        for s in range(8):
            tiles[pl.ds(n * NZ * 8 + s, NZ, stride=8), :] = total[:, s * 128 : (s + 1) * 128]
        for qq in range(NQ):
            for half in range(NB // 2):
                two = [tiles[pl.ds((n * NZ + NQ * (2 * half + k) + qq) * 8, 8), :] for k in range(2)]
                pieces[pl.ds((n * NQ + qq) * PIECE + half * 16, 16), :] = jnp.concatenate(two, axis=0).astype(BF16)

    wait_for(dense_own, load_sem.at[1])
    dense_pair.wait_recv()
    for n in range(NX):
        sum_column(n)

    @pl.when(c == 1)
    def _():
        pl.semaphore_wait(barrier, 2 * len(greeted))
        pl.semaphore_signal(all_in_kernel, inc=1, device_id=pair, device_id_type=MESH)

    @pl.when(c == 0)
    def _():
        pl.semaphore_wait(all_in_kernel, 1)

    to_near = [
        send(
            pieces.at[at(((x + dx) % NX * NQ + along(dz) % NQ) * PIECE, PIECE, 32)],
            near_in.at[pl.ds(k * PIECE, PIECE)],
            near_sem.at[0], near_sem.at[1 if k < FIRST else 2], near[k],
        )
        for k, (dx, dz) in enumerate(NEAR)
    ]
    for copy in to_near:
        copy.start()

    pl.semaphore_signal(known, inc=1, device_id=far[0], device_id_type=MESH)
    wait_for(own_states, load_sem.at[4])
    to_states = [send(own_states, own_states, far_sem.at[0], far_sem.at[1], far[d]) for d in range(NB - 1)]
    to_states[0].start()
    to_states[2].start()

    block_pair.wait_recv()

    def cross_step(i, carry):
        off = pl.multiple_of(i * 32, 32)
        own = scale(2 * (1 - xh) + c, off)
        other = pair_in[pl.ds(pl.multiple_of(ROWS + off, 32), 32)]
        cross_send[pl.ds(off, 32)] = (own.astype(F32) + other.astype(F32)).astype(BF16)
        return carry

    lax.fori_loop(0, ROWS // 32, cross_step, 0)
    pl.semaphore_wait(known, 1)
    to_states[1].start()
    to_cross = send(cross_send, cross_in, cross_sem.at[0], cross_sem.at[1], cross)

    total = [tiles[at((x * NZ + NQ * b + q) * 8, 8, 8), :] for b in range(NB)]
    total = jnp.concatenate(total, axis=0)
    wait_for(near_in.at[pl.ds(FIRST * PIECE, (len(NEAR) - FIRST) * PIECE)], near_sem.at[2])
    to_cross.start()
    for k in range(FIRST, len(NEAR)):
        total = total + near_in[pl.ds(k * PIECE, PIECE), :].astype(F32)
    wait_for(near_in.at[pl.ds(0, FIRST * PIECE)], near_sem.at[1])
    for k in range(FIRST):
        total = total + near_in[pl.ds(k * PIECE, PIECE), :].astype(F32)
    far_own = far_buf.at[at(zb * PIECE, PIECE, 32)]
    far_own[...] = total.astype(BF16)
    to_far = [send(far_own, far_own, far_sem.at[2], far_sem.at[3], far[d]) for d in (1, 0, 2)]
    for copy in to_far:
        copy.start()

    wait_for(states, load_sem.at[5])
    dense_pair.wait_send()
    block_pair.wait_send()
    wait_for(near_in, near_sem.at[0])
    to_cross.wait_recv()

    def update_step(i, carry):
        off = pl.multiple_of(i * 32, 32)
        rows = pl.ds(off, 32)
        own = scale(dp, off)
        gradient = own.astype(F32) + pair_in[rows].astype(F32) + cross_in[rows].astype(F32)
        new, moment_new, second_new = adam_update(states[0, rows], states[1, rows], states[2, rows], gradient)
        master_out[rows] = new
        moment_out[rows] = moment_new
        second_out[rows] = second_new
        weight_out[pl.ds(pl.multiple_of(dp * ROWS + off, 32), 32)] = new.astype(BF16)
        return carry

    lax.fori_loop(0, ROWS // 32, update_step, 0)
    own_weight = weight_out.at[at(dp * ROWS, ROWS, 32)]
    weight_cross = send(own_weight, own_weight, cross_sem.at[2], cross_sem.at[3], cross)
    weight_cross.start()
    weight_pair = send(own_weight, own_weight, cross_sem.at[2], cross_sem.at[4], pair)
    weight_pair.start()

    wait_for(dstates.at[pl.ds(0, 72)], far_sem.at[0])
    wait_for(dstates.at[pl.ds(0, 72)], far_sem.at[1])
    to_cross.wait_send()
    wait_for(far_buf.at[pl.ds(0, 3 * PIECE)], far_sem.at[3])
    dense_sum = jnp.zeros((PIECE, 128), F32)
    for b in range(NB):
        dense_sum = dense_sum + far_buf[pl.ds(b * PIECE, PIECE), :].astype(F32)
    news = []
    for b in range(NB):
        old = [dstates[pl.ds(b * 24 + 8 * i, 8), :] for i in range(3)]
        new = adam_update(*old, dense_sum[b * 8 : (b + 1) * 8])
        for i in range(3):
            dnew[pl.ds(b * 24 + 8 * i, 8), :] = new[i]
        news.append(new[0])
    own_piece = dweights.at[at(c * 512 + (x * NQ + q) * PIECE, PIECE, 32)]
    own_piece[...] = jnp.concatenate(news, axis=0).astype(BF16)
    to_gather = [
        send(own_piece, own_piece, gather_sem.at[0], gather_sem.at[1 + dx], near[k])
        for k, (dx, dz) in enumerate(NEAR)
    ]
    for copy in to_gather:
        copy.start()
    for i, ref in enumerate((dmaster_out, dmoment_out, dsecond_out)):
        ref[...] = dnew[at(zb * 24 + 8 * i, 8, 8), :]
    wait_for(far_buf.at[pl.ds(0, 3 * PIECE)], far_sem.at[2])

    weight_cross.wait_recv()
    cross_weight = weight_out.at[at((2 * (1 - xh) + c) * ROWS, ROWS, 32)]
    weight_on = send(cross_weight, cross_weight, cross_sem.at[2], cross_sem.at[4], pair)
    weight_on.start()

    def place(core, column, slot):
        first = pl.multiple_of(core * 512 + column * NQ * PIECE, 128)
        for qq in range(NQ):
            piece = dweights[pl.ds(pl.multiple_of(first + qq * PIECE, 32), PIECE), :].astype(F32)
            for b in range(NB):
                spread[pl.ds((slot * NZ + NQ * b + qq) * 8, 8), :] = piece[b * 8 : (b + 1) * 8]
        to = dense_rows(column, core)
        for s in range(8):
            row = spread[pl.ds(slot * NZ * 8 + s, NZ, stride=8), :]
            dweight_out[to, s * 128 : (s + 1) * 128] = row.astype(BF16)

    order = (0, 1, 3, 2)
    for dx in order:
        column = (x + NX - dx) % NX
        pieces_in = NQ - 1 if dx == 0 else NQ
        wait_for(dweights.at[pl.ds(0, pieces_in * PIECE)], gather_sem.at[1 + dx])
        group = dweights.at[at(c * 512 + column * NQ * PIECE, NQ * PIECE, 128)]
        send(group, group, back_sem.at[0], back_sem.at[1 if dx != 2 else 2], pair).start()
        place(c, column, dx)
    wait_for(near_in, gather_sem.at[0])
    wait_for(weight_out.at[pl.ds(0, 3 * ROWS)], cross_sem.at[2])
    wait_for(weight_out.at[pl.ds(0, 2 * ROWS)], cross_sem.at[4])
    wait_for(dweights.at[pl.ds(0, 3 * NQ * PIECE)], back_sem.at[1])
    for dx in order[:3]:
        place(1 - c, (x + NX - dx) % NX, 4 + dx)
    wait_for(dweights.at[pl.ds(0, NQ * PIECE)], back_sem.at[2])
    place(1 - c, (x + 2) % NX, 6)
    wait_for(dweights.at[pl.ds(0, 4 * NQ * PIECE)], back_sem.at[0])


def store(*refs):
    sources, outs, sem = refs[:8], refs[8:16], refs[16]
    copies = [pltpu.make_async_copy(s, o, sem.at[i]) for i, (s, o) in enumerate(zip(sources, outs))]
    for copy in copies:
        copy.start()
    for copy in copies:
        copy.wait()


def shards(
    expert_partials,
    token_counts,
    expert_master,
    expert_moment,
    expert_second,
    dense_partials,
    dense_master,
    dense_moment,
    dense_second,
):
    hbm = pl.BlockSpec(memory_space=pltpu.HBM)
    vmem = pl.BlockSpec(memory_space=pltpu.VMEM)
    dma = pltpu.SemaphoreType.DMA
    shapes = [
        ((4 * ROWS, COLS), BF16),
        ((ROWS, COLS), F32),
        ((ROWS, COLS), F32),
        ((ROWS, COLS), F32),
        ((128, 1024), BF16),
        ((8, 128), F32),
        ((8, 128), F32),
        ((8, 128), F32),
    ]
    results = pl.pallas_call(
        exchange,
        out_shape=[pltpu.VMEM(s, d) for s, d in shapes],
        in_specs=[hbm] * 9,
        out_specs=[vmem] * 8,
        scratch_shapes=[
            pltpu.SMEM((1, 4), jnp.int32),
            pltpu.VMEM((4 * ROWS, COLS), BF16),
            pltpu.VMEM((3, ROWS, COLS), F32),
            pltpu.VMEM((2 * ROWS, COLS), BF16),
            pltpu.VMEM((2 * ROWS, COLS), BF16),
            pltpu.VMEM((ROWS, COLS), BF16),
            pltpu.VMEM((ROWS, COLS), BF16),
            pltpu.VMEM((64, 1024), BF16),
            pltpu.VMEM((64, 1024), BF16),
            pltpu.VMEM((64, 1024), BF16),
            pltpu.VMEM((512, 128), F32),
            pltpu.VMEM((512, 128), BF16),
            pltpu.VMEM((len(NEAR) * PIECE, 128), BF16),
            pltpu.VMEM((NB * PIECE, 128), BF16),
            pltpu.VMEM((NB * 24, 128), F32),
            pltpu.VMEM((NB * 24, 128), F32),
            pltpu.VMEM((1024, 128), BF16),
            pltpu.VMEM((1024, 128), F32),
            dma((6,)),
            dma((4,)),
            dma((3,)),
            dma((4,)),
            dma((5,)),
            dma((5,)),
            dma((3,)),
            pltpu.SemaphoreType.REGULAR,
            pltpu.SemaphoreType.REGULAR,
            pltpu.SemaphoreType.REGULAR,
        ],
        compiler_params=pltpu.CompilerParams(
            collective_id=0, has_side_effects=True, vmem_limit_bytes=56 * 2**20
        ),
        name="exchange",
    )(
        expert_partials.reshape(4 * ROWS, COLS),
        token_counts,
        expert_master,
        expert_moment,
        expert_second,
        dense_partials.reshape(128, 1024),
        dense_master.reshape(8, 128),
        dense_moment.reshape(8, 128),
        dense_second.reshape(8, 128),
    )
    outs = pl.pallas_call(
        store,
        out_shape=[jax.ShapeDtypeStruct(s, d) for s, d in shapes],
        in_specs=[vmem] * 8,
        out_specs=[hbm] * 8,
        scratch_shapes=[dma((8,))],
        compiler_params=pltpu.CompilerParams(vmem_limit_bytes=8 * 2**20),
        name="store",
    )(*results)
    outs = list(outs)
    outs[4] = outs[4].reshape(128, 1, 1024)
    for i in (5, 6, 7):
        outs[i] = outs[i].reshape(1024)
    return tuple(outs)


def solution(mesh):
    return jax.shard_map(
        shards,
        mesh=mesh,
        in_specs=(
            P("dp", "expert", "tensor"),
            P("dp", None),
            P(("expert", "dp"), "tensor"),
            P(("expert", "dp"), "tensor"),
            P(("expert", "dp"), "tensor"),
            P(("dp", "expert"), None, "tensor", None),
            P(("dp", "expert", "tensor")),
            P(("dp", "expert", "tensor")),
            P(("dp", "expert", "tensor")),
        ),
        out_specs=(
            P("expert", "tensor"),
            P(("expert", "dp"), "tensor"),
            P(("expert", "dp"), "tensor"),
            P(("expert", "dp"), "tensor"),
            P(None, "tensor", None),
            P(("dp", "expert", "tensor")),
            P(("dp", "expert", "tensor")),
            P(("dp", "expert", "tensor")),
        ),
        check_vma=False,
    )
```
